512 devices in a mesh: row: 8 (over x, core), col: 8 (over z), rep: 8 (over y).
Axes of the slice: x: 4, y: 8, z: 8, core: 2. Of those that a mesh axis runs over, the one named last changes fastest.
Arguments:
- m_tensor: bfloat16 [512, 256, 256], P('row', ('col', 'rep')), may hold values from -1 to 1
- green: bfloat16 [2, 256, 256], P(None, ('row', 'col')), may hold values from -0.375 to 0.375
- tile_mask: int32 [4, 2, 2], replicated, may hold values 0 or 1
- green_mask: int32 [2, 2, 2], replicated, may hold values 0 or 1
Outputs:
- chi_cyclic: float32 [512, 512], P('row', ('col', 'rep'))
The draws below stay inside these ranges and needn't reach their ends.
All inputs are finite; a program needn't handle non-finite values.
Results may differ from the reference program's by a relative error of at most 0.0041.
Values may be sent and summed in bfloat16 or wider, within the bound.
No kernel may reach another device: no remote copies, remote signals or barrier semaphores. Data moves between devices by JAX's collectives and lax.ppermute only.
A program may use at most 64 MiB of HBM per device.

```python
import jax
import jax.numpy as jnp
from jax import lax

NAO = 256
TILE = 128
RI_ROW = 64
NRI = 512
AT = 2
RT = 4
N_ROW = 8


def place_ends(array, key, low, largest):
    longest = array.shape.index(max(array.shape))
    spots = []
    for shift in (0, 1):
        where = [jax.random.randint(jax.random.fold_in(key, axis), (), 0, length) for axis, length in enumerate(array.shape)]
        where[longest] = (where[longest] + shift) % array.shape[longest]
        spots.append(tuple(where))
    return array.at[spots[0]].set(low).at[spots[1]].set(largest)


def block_levels(own_key, dims, pieces, low, high):
    factor_of, own = 1.0, jax.random.fold_in(own_key, 6)
    for position, parts in pieces:
        steps = jnp.exp(jax.random.uniform(jax.random.fold_in(own, position), (parts,), jnp.float32, low / len(pieces), high / len(pieces)))
        factor_of = factor_of * jnp.repeat(steps, dims[position] // parts).reshape([-1 if axis == position else 1 for axis in range(len(dims))])
    return factor_of


def normal_values(stream_key, extent, width, bound, shards=(), dtype=jnp.bfloat16):
    factor_of = block_levels(stream_key, extent, shards, -0.22, 0.18) if shards else 1.0
    drawn = jax.random.normal(stream_key, extent, jnp.float32) * width * factor_of
    return jnp.minimum(jnp.maximum(drawn, -bound), bound).astype(dtype)


def setup_inputs(seed: int = 0) -> dict:
    keys = jax.random.split(jax.random.key(seed), 5)
    m_tensor = normal_values(keys[0], (NRI, NAO, NAO), (NAO ** -0.5), 1.0, ((0, 8), (1, 64)))
    green = normal_values(keys[1], (2, NAO, NAO), NAO ** -0.5, 0.375, ((1, 64),))
    tile_mask = place_ends((jax.random.randint(keys[2], (RT, AT, AT), 0, 4) < 3).astype(jnp.int32), jax.random.fold_in(keys[2], 1), 0, 1)
    green_mask = place_ends((jax.random.randint(keys[3], (2, AT, AT), 0, 4) < 3).astype(jnp.int32), jax.random.fold_in(keys[3], 1), 0, 1)
    return dict(m_tensor=m_tensor, green=green, tile_mask=tile_mask, green_mask=green_mask)


def reference(m_tensor, green, tile_mask, green_mask):
    total_ri = m_tensor.shape[0]
    ri_tiles = total_ri // TILE
    ao_tiles = NAO // TILE
    green_keep = jnp.repeat(jnp.repeat(green_mask.astype(jnp.bfloat16), TILE, axis=1), TILE, axis=2)
    kept_green = green * green_keep
    occupied = kept_green[0]
    virtual = kept_green[1]
    tile_keep = tile_mask.astype(jnp.bfloat16)
    masked = m_tensor.reshape(ri_tiles, TILE, ao_tiles, TILE, ao_tiles, TILE)
    masked = (masked * tile_keep[:, None, :, None, :, None]).reshape(total_ri, NAO, NAO)

    def contract_one(matrix):
        halfway = jnp.dot(matrix, virtual, preferred_element_type=jnp.float32).astype(jnp.bfloat16)
        return jnp.dot(occupied.T, halfway, preferred_element_type=jnp.float32).astype(jnp.bfloat16)

    contracted = lax.map(contract_one, masked)
    left_side = contracted.reshape(total_ri, NAO * NAO).astype(jnp.float32)
    right_side = masked.reshape(total_ri, NAO * NAO).astype(jnp.float32)
    chi = jnp.dot(left_side, right_side.T, precision=lax.Precision.HIGHEST, preferred_element_type=jnp.float32)
    block_rows = RI_ROW // N_ROW
    chi_cyclic = chi.reshape(N_ROW, N_ROW, block_rows, total_ri).transpose(1, 0, 2, 3).reshape(total_ri, total_ri)
    return chi_cyclic
```

```python
import jax
import jax.numpy as jnp
from jax import lax
from jax.sharding import PartitionSpec as P

TILE = 128
GRID = ("col", "rep")


def body(m_tensor, green, tile_mask, green_mask):
    row_count, mu_block, ao_count = m_tensor.shape
    groups = lax.axis_size(GRID)
    rows = lax.axis_size("row")
    cells = lax.axis_size(("row", "col"))
    sent = jnp.broadcast_to(green[None], (cells,) + green.shape)
    whole = lax.all_to_all(sent, ("row", "col"), 0, 0, tiled=True)
    whole = whole.transpose(1, 0, 2, 3).reshape(2, ao_count, ao_count)
    green_keep = jnp.repeat(jnp.repeat(green_mask.astype(jnp.bfloat16), TILE, axis=1), TILE, axis=2)
    whole = whole * green_keep
    occupied, virtual = whole[0], whole[1]
    keep_two = tile_mask[
        lax.axis_index("row") * row_count // TILE, lax.axis_index(GRID) * mu_block // TILE
    ]
    keep = jnp.repeat(keep_two.astype(jnp.bfloat16), TILE)
    masked = m_tensor * keep[None, None, :]
    m_all = lax.all_gather(masked.reshape(row_count, mu_block * ao_count), "row", axis=0, tiled=True)
    mine = lax.all_to_all(masked, GRID, 0, 0, tiled=True).reshape(ao_count, ao_count)
    halfway = jnp.dot(mine, virtual, preferred_element_type=jnp.float32).astype(jnp.bfloat16)
    product = lax.dot_general(
        occupied, halfway, (((0,), (0,)), ((), ())), preferred_element_type=jnp.float32
    ).astype(jnp.bfloat16)
    contracted = lax.all_to_all(
        product.reshape(groups, mu_block, ao_count), GRID, 0, 0, tiled=True
    ).reshape(row_count, mu_block * ao_count)
    partial = lax.dot_general(
        m_all, contracted, (((1,), (1,)), ((), ())), preferred_element_type=jnp.float32
    )
    width = partial.shape[0] // groups
    pieces = lax.all_to_all(partial.reshape(groups, width, row_count), GRID, 0, 0, tiled=True)
    summed = jnp.sum(pieces, axis=0)
    blocks = summed.reshape(width, rows, row_count // rows).transpose(1, 2, 0)
    result = lax.all_to_all(blocks, "row", 0, 0, tiled=True)
    return result.reshape(row_count, width)


def solution(mesh):
    return jax.shard_map(
        body,
        mesh=mesh,
        in_specs=(P("row", ("col", "rep"), None), P(None, ("row", "col"), None), P(), P()),
        out_specs=P("row", ("col", "rep")),
        check_vma=False,
    )
```

```python
import jax
import jax.numpy as jnp
from jax import lax
from jax.sharding import PartitionSpec as P

TILE = 128
GRID = ("col", "rep")


def swap_pairs(size):
    return [(a * size + b, b * size + a) for a in range(size) for b in range(size)]


def body(m_tensor, green, tile_mask, green_mask):
    row_count, mu_block, ao_count = m_tensor.shape
    groups = lax.axis_size(GRID)
    rows = lax.axis_size("row")
    chips = rows // 2
    halves = ao_count // TILE
    row, col = lax.axis_index("row"), lax.axis_index("col")

    own = m_tensor.reshape(row_count, mu_block, halves, TILE).transpose(0, 2, 1, 3)
    own = own.reshape(row_count, halves * mu_block, TILE)
    green_own = green.reshape(2, mu_block, halves, TILE).transpose(0, 2, 1, 3)
    green_own = green_own.reshape(2 * halves * mu_block, TILE)
    m_turned = lax.ppermute(own, ("row", "col"), swap_pairs(rows))
    green_turned = lax.ppermute(green_own, ("col", "rep"), swap_pairs(rows))

    mu_tile = lax.axis_index(GRID) * mu_block // TILE
    keep_own = jnp.repeat(tile_mask[row * row_count // TILE, mu_tile].astype(jnp.bfloat16), TILE)
    right = (m_tensor * keep_own[None, None, :]).reshape(row_count, mu_block * ao_count)
    pieces = [right]
    for step in range(1, chips):
        pairs = [(r, (r + 2 * step) % rows) for r in range(rows)]
        pieces.append(lax.ppermute(right, "row", pairs))
    near = jnp.concatenate(pieces, axis=0)
    far = lax.ppermute(near, "row", [(r, r ^ 1) for r in range(rows)])

    sent = jnp.concatenate(
        [own_part for own_part in (m_turned, jnp.broadcast_to(green_turned[None], (groups,) + green_turned.shape))],
        axis=1,
    )
    got = lax.all_to_all(sent, ("row", "rep"), 0, 0, tiled=True)
    got = got.reshape(groups, 3, halves, mu_block, TILE).transpose(1, 0, 3, 2, 4)
    got = got.reshape(3, ao_count, ao_count)
    tile_keep = jnp.repeat(jnp.repeat(tile_mask[col * row_count // TILE].astype(jnp.bfloat16), TILE, axis=0), TILE, axis=1)
    green_keep = jnp.repeat(jnp.repeat(green_mask.astype(jnp.bfloat16), TILE, axis=1), TILE, axis=2)
    mine = got[0] * tile_keep
    occupied = got[1] * green_keep[0]
    virtual = got[2] * green_keep[1]
    halfway = jnp.dot(mine, virtual, preferred_element_type=jnp.float32).astype(jnp.bfloat16)
    product = lax.dot_general(
        occupied, halfway, (((0,), (0,)), ((), ())), preferred_element_type=jnp.float32
    ).astype(jnp.bfloat16)
    contracted = lax.all_to_all(
        product.reshape(groups, mu_block, ao_count), GRID, 0, 0, tiled=True
    ).reshape(row_count, mu_block * ao_count)

    pair_dims = (((1,), (1,)), ((), ()))
    width = rows * row_count // groups
    partial = jnp.zeros((rows, row_count, row_count), jnp.float32)
    for held, core in ((near, row % 2), (far, 1 - row % 2)):
        part = lax.dot_general(held, contracted, pair_dims, preferred_element_type=jnp.float32)
        part = part.reshape(chips, row_count, row_count)
        for step in range(chips):
            block = (row // 2 - step + chips) % chips * 2 + core
            partial = lax.dynamic_update_slice(partial, part[step][None], (block, 0, 0))
    slices = lax.all_to_all(partial.reshape(groups, width, row_count), GRID, 0, 0, tiled=True)
    return jnp.sum(slices, axis=0).T


def solution(mesh):
    return jax.shard_map(
        body,
        mesh=mesh,
        in_specs=(P("row", ("col", "rep"), None), P(None, ("row", "col"), None), P(), P()),
        out_specs=P("row", ("col", "rep")),
        check_vma=False,
    )
```

```python
import jax
import jax.numpy as jnp
from jax import lax
from jax.sharding import PartitionSpec as P

TILE = 128
GRID = ("col", "rep")


def body(m_tensor, green, tile_mask, green_mask):
    row_count, mu_block, ao_count = m_tensor.shape
    groups = lax.axis_size(GRID)
    rows = lax.axis_size("row")
    chips = rows // 2
    halves = ao_count // TILE
    line = halves * mu_block
    row, col, rep = lax.axis_index("row"), lax.axis_index("col"), lax.axis_index("rep")

    own = m_tensor.reshape(row_count, mu_block, halves, TILE).transpose(0, 2, 1, 3)
    own = own.reshape(rows, row_count // rows * line, TILE)
    green_own = green.reshape(2, mu_block, halves, TILE).transpose(0, 2, 1, 3)
    green_own = green_own.reshape(1, 2 * line, TILE)
    first = jnp.concatenate([own, jnp.broadcast_to(green_own, (rows, 2 * line, TILE))], axis=1)
    first = lax.all_to_all(first, "row", 0, 0, tiled=True)
    cyclic = first[:, : row_count // rows * line].reshape(groups, line, TILE)
    shard = lax.dynamic_slice_in_dim(first[:, row_count // rows * line :], rep, 1, axis=0)
    sent = jnp.concatenate([cyclic, jnp.broadcast_to(shard, (groups, 2 * line, TILE))], axis=1)

    mu_tile = lax.axis_index(GRID) * mu_block // TILE
    keep_own = jnp.repeat(tile_mask[row * row_count // TILE, mu_tile].astype(jnp.bfloat16), TILE)
    right = (m_tensor * keep_own[None, None, :]).reshape(row_count, mu_block * ao_count)

    def along(step):
        return lax.ppermute(right, "row", [(r, (r + 2 * step) % rows) for r in range(rows)])

    right, sent = lax.optimization_barrier((right, sent))
    got = lax.all_to_all(sent, GRID, 0, 0, tiled=True)
    got = got.reshape(groups, 3, halves, mu_block, TILE)
    mine = got[:, 0].transpose(0, 2, 1, 3).reshape(ao_count, ao_count)
    whole = got[:, 1:].reshape(groups // rows, rows, 2, halves, mu_block, TILE)
    whole = whole.transpose(2, 1, 0, 4, 3, 5).reshape(2, ao_count, ao_count)
    tile_keep = jnp.repeat(jnp.repeat(tile_mask[col * row_count // TILE].astype(jnp.bfloat16), TILE, axis=0), TILE, axis=1)
    green_keep = jnp.repeat(jnp.repeat(green_mask.astype(jnp.bfloat16), TILE, axis=1), TILE, axis=2)
    mine = mine * tile_keep
    whole = whole * green_keep
    halfway = jnp.dot(mine, whole[1], preferred_element_type=jnp.float32).astype(jnp.bfloat16)
    product = lax.dot_general(
        whole[0], halfway, (((0,), (0,)), ((), ())), preferred_element_type=jnp.float32
    ).astype(jnp.bfloat16)
    near = jnp.concatenate([right] + [along(step) for step in (1, 2, 3)], axis=0)
    near, product = lax.optimization_barrier((near, product))
    far = lax.ppermute(near, "row", [(r, r ^ 1) for r in range(rows)])
    contracted = lax.all_to_all(
        product.reshape(groups, mu_block, ao_count), GRID, 0, 0, tiled=True
    ).reshape(row_count, mu_block * ao_count)

    pair_dims = (((1,), (1,)), ((), ()))
    width = rows * row_count // groups
    partial = jnp.zeros((chips, 2, row_count, row_count), jnp.float32)
    for held, core in ((near, row % 2), (far, 1 - row % 2)):
        part = lax.dot_general(held, contracted, pair_dims, preferred_element_type=jnp.float32)
        part = part.reshape(chips, row_count, row_count)
        for step in range(chips):
            chip = (row // 2 - step + chips) % chips
            partial = lax.dynamic_update_slice(partial, part[step][None, None], (chip, core, 0, 0))
    slices = lax.all_to_all(partial.reshape(groups, width, row_count), GRID, 0, 0, tiled=True)
    return jnp.sum(slices, axis=0).T


def solution(mesh):
    return jax.shard_map(
        body,
        mesh=mesh,
        in_specs=(P("row", ("col", "rep"), None), P(None, ("row", "col"), None), P(), P()),
        out_specs=P("row", ("col", "rep")),
        check_vma=False,
    )
```

```python
import jax
import jax.numpy as jnp
import numpy as np
from jax import lax
from jax.experimental import pallas as pl
from jax.experimental.pallas import tpu as pltpu
from jax.sharding import PartitionSpec as P

TILE = 128
COST_F = 10**10
COST_A = 5 * 10**9
COST_1 = 1
GRID = ("col", "rep")
LINE = 8
BF16 = jnp.bfloat16
F32 = jnp.float32
VMEM = pl.BlockSpec(memory_space=pltpu.VMEM)
SMEM = pl.BlockSpec(memory_space=pltpu.SMEM)
NN = (((1,), (0,)), ((), ()))
NT = (((1,), (1,)), ((), ()))
TN = (((0,), (0,)), ((), ()))


def held(array):
    return pltpu.with_memory_space_constraint(array, pltpu.VMEM)


def dot(left, right, dims=NN):
    return lax.dot_general(left, right, dims, preferred_element_type=F32)


def pick(index):
    index = np.asarray(index)
    return jnp.asarray(index[:, None] == np.arange(index.size)[None, :], BF16)


def orders(groups):
    size = groups * LINE
    row = np.arange(size)
    half, place = row // (size // 2), row % (size // 2)
    block, inner = place // 4, place % 4
    natural = block * LINE + half * 4 + inner
    turned = (block % 8 * 8 + block // 8) * LINE + half * 4 + inner
    part, func = row // groups, row % groups
    return natural, turned, func * LINE + part % 2 * 4 + part // 2


def first_kernel(tile_ref, green_ref, m_ref, shard_ref, out_ref):
    tile, mu_tile = lax.axis_index("row") // 2, lax.axis_index("col") // 4
    green_tile = lax.axis_index("row") // 4
    length = m_ref.shape[1]

    def halves(count, low, high):
        line = lax.broadcasted_iota(jnp.int32, (count, TILE), 0) % LINE
        return jnp.where(line < 4, low.astype(F32), high.astype(F32))

    keep = halves(length, tile_ref[mu_tile, 0, tile], tile_ref[mu_tile, 1, tile])
    for k in range(out_ref.shape[0]):
        out_ref[k, :length] = (m_ref[k].astype(F32) * keep).astype(BF16)
    keep_green = jnp.concatenate(
        [halves(LINE, green_ref[w, green_tile, 0], green_ref[w, green_tile, 1]) for w in range(2)], axis=0
    )
    shard = (shard_ref[...].astype(F32) * keep_green).astype(BF16)
    for k in range(out_ref.shape[0]):
        out_ref[k, length:] = shard


def second_kernel(got_ref, out_ref):
    rows = got_ref.shape[0]
    groups = out_ref.shape[0]
    length = groups // rows * LINE
    out_ref[:, :LINE] = got_ref[:, :length].reshape(groups, LINE, TILE)
    shard = got_ref[lax.axis_index("rep"), length:]
    out_ref[:, LINE:] = jnp.broadcast_to(shard[None], (groups,) + shard.shape)


def product_kernel(natural_ref, turned_ref, got_ref, out_ref):
    groups = got_ref.shape[0]
    size = groups * LINE
    side = size // 2
    got = got_ref[...]
    m_part = got[:, :LINE].reshape(size, TILE)
    o_part = got[:, LINE : 2 * LINE].reshape(size, TILE)
    v_part = got[:, 2 * LINE :].reshape(size, TILE)
    natural = natural_ref[...]
    turned = turned_ref[...]

    def square(rows):
        rows = rows.astype(BF16)
        return jnp.concatenate([rows[:side], rows[side:]], axis=1)

    virtual = square(dot(turned, v_part))
    mine = square(dot(natural, m_part))
    occupied = square(dot(turned, o_part))
    halfway = dot(mine, virtual).astype(BF16)
    wide = dot(occupied, natural[:side] + natural[side:]).astype(BF16)
    product = dot(wide, halfway, TN)
    line = lax.broadcasted_iota(jnp.int32, (size, TILE), 0) % LINE
    out = jnp.where(line < 4, product[:, :TILE], product[:, TILE:]).astype(BF16)
    out_ref[...] = out.reshape(groups, LINE, TILE)


def near_kernel(order_ref, y_ref, near_ref, out_ref, flat_ref):
    count = y_ref.shape[0]
    picked = dot(order_ref[...], y_ref[...].reshape(count * LINE, TILE)).astype(BF16)
    flat = jnp.concatenate([picked[b * count : (b + 1) * count] for b in range(LINE)], axis=1)
    flat_ref[...] = flat
    place(flat, near_ref, out_ref, lax.axis_index("row") % 2)


def far_kernel(flat_ref, far_ref, part_ref, out_ref):
    out_ref[...] = part_ref[...]
    place(flat_ref[...], far_ref, out_ref, 1 - lax.axis_index("row") % 2)


def place(flat, held_ref, out_ref, parity):
    count = flat.shape[0]
    chip = lax.axis_index("row") // 2
    part = dot(held_ref[...], flat, NT)
    for step in range(4):
        rows = part[step * count : (step + 1) * count]
        wide = jnp.concatenate([rows[: count // 2], rows[count // 2 :]], axis=1)
        block = lax.rem(chip - step + 4, 4) * 2 + parity
        start = pl.multiple_of(block * (count // 2), count // 2)
        out_ref[pl.ds(start, count // 2), :] = wide


def gather_kernel(*refs):
    count = refs[0].shape[0]
    for step, ref in enumerate(refs[:-1]):
        refs[-1][step * count : (step + 1) * count] = ref[...]


def cost(flops):
    return pl.CostEstimate(flops=flops, bytes_accessed=0, transcendentals=0)


def sum_kernel(got_ref, out_ref):
    size = got_ref.shape[0]
    total = jnp.sum(got_ref[...].reshape(size // 8, 8, TILE), axis=0)
    total = total[:4] + total[4:]
    out_ref[...] = jnp.concatenate([total[:, :64], total[:, 64:]], axis=0)


def body(m_tensor, green, tile_mask, green_mask):
    row_count, mu_block, ao_count = m_tensor.shape
    groups = lax.axis_size(GRID)
    rows = lax.axis_size("row")
    halves = ao_count // TILE
    line = halves * mu_block
    row = lax.axis_index("row")
    natural, turned, flat_order = (pick(order) for order in orders(groups))

    own = m_tensor.reshape(row_count, mu_block, halves, TILE).transpose(0, 2, 1, 3)
    own = own.reshape(rows, row_count // rows * line, TILE)
    green_own = green.reshape(2, mu_block, halves, TILE).transpose(0, 2, 1, 3)
    green_own = green_own.reshape(2 * line, TILE)
    first = pl.pallas_call(
        first_kernel,
        out_shape=pltpu.VMEM((rows, row_count // rows * line + 2 * line, TILE), BF16),
        in_specs=[SMEM, SMEM, VMEM, VMEM],
        out_specs=VMEM,
    )(tile_mask.transpose(1, 2, 0), green_mask, own, green_own)
    first = lax.all_to_all(first, "row", 0, 0, tiled=True)
    sent = pl.pallas_call(
        second_kernel,
        out_shape=pltpu.VMEM((groups, 3 * line, TILE), BF16),
        in_specs=[VMEM],
        out_specs=VMEM,
    )(held(first))

    mu_tile = lax.axis_index(GRID) * mu_block // TILE
    keep_own = jnp.repeat(tile_mask[row * row_count // TILE, mu_tile].astype(BF16), TILE)
    right = m_tensor * keep_own[None, None, :]
    right = right.reshape(rows, 2, row_count // rows // 2, mu_block * ao_count).transpose(1, 0, 2, 3)
    right = right.reshape(row_count, mu_block * ao_count)

    def along(step):
        return lax.ppermute(right, "row", [(r, (r + 2 * step) % rows) for r in range(rows)])

    right, sent = lax.optimization_barrier((right, sent))
    got = lax.all_to_all(sent, GRID, 0, 0, tiled=True)
    product = pl.pallas_call(
        product_kernel,
        out_shape=pltpu.VMEM((groups, line, TILE), BF16),
        in_specs=[VMEM, VMEM, VMEM],
        out_specs=VMEM,
        cost_estimate=cost(COST_1),
    )(held(natural), held(turned), held(got))
    near = pl.pallas_call(
        gather_kernel,
        out_shape=pltpu.VMEM((4 * row_count, mu_block * ao_count), BF16),
        in_specs=[VMEM] * 4,
        out_specs=VMEM,
        cost_estimate=cost(COST_F),
    )(held(right), *[held(along(step)) for step in (1, 2, 3)])
    far = lax.ppermute(near, "row", [(r, r ^ 1) for r in range(rows)])
    contracted = lax.all_to_all(product, GRID, 0, 0, tiled=True)
    partial, flat = pl.pallas_call(
        near_kernel,
        out_shape=(pltpu.VMEM((groups * 4, TILE), F32), pltpu.VMEM((row_count, mu_block * ao_count), BF16)),
        in_specs=[VMEM, VMEM, VMEM],
        out_specs=(VMEM, VMEM),
        cost_estimate=cost(COST_A),
    )(held(flat_order), held(contracted), held(near))
    partial = pl.pallas_call(
        far_kernel,
        out_shape=pltpu.VMEM((groups * 4, TILE), F32),
        in_specs=[VMEM, VMEM, VMEM],
        out_specs=VMEM,
    )(held(flat), held(far), held(partial))
    slices = lax.all_to_all(partial.reshape(groups, 4, TILE), GRID, 0, 0, tiled=True)
    result = pl.pallas_call(
        sum_kernel,
        out_shape=jax.ShapeDtypeStruct((8, row_count), F32),
        in_specs=[VMEM],
        out_specs=VMEM,
    )(held(slices.reshape(groups * 4, TILE)))
    return result.T


def solution(mesh):
    return jax.shard_map(
        body,
        mesh=mesh,
        in_specs=(P("row", ("col", "rep"), None), P(None, ("row", "col"), None), P(), P()),
        out_specs=P("row", ("col", "rep")),
        check_vma=False,
    )
```

```python
import jax
import jax.numpy as jnp
import numpy as np
from jax import lax
from jax.experimental import pallas as pl
from jax.experimental.pallas import tpu as pltpu
from jax.sharding import PartitionSpec as P

TILE = 128
FIRST = (4, 4)
SECOND = (4, 4)
THIRD = (4, 4)
ROWS = 1
COST_F = 10**10
COST_A = 10**9
COST_1 = 1
COST_G = 10**10
GRID = ("col", "rep")
LINE = 8
BF16 = jnp.bfloat16
F32 = jnp.float32
VMEM = pl.BlockSpec(memory_space=pltpu.VMEM)
SMEM = pl.BlockSpec(memory_space=pltpu.SMEM)
NN = (((1,), (0,)), ((), ()))
NT = (((1,), (1,)), ((), ()))
TN = (((0,), (0,)), ((), ()))


def held(array):
    return pltpu.with_memory_space_constraint(array, pltpu.VMEM)


def dot(left, right, dims=NN):
    return lax.dot_general(left, right, dims, preferred_element_type=F32)


def pick(index):
    index = np.asarray(index)
    return jnp.asarray(index[:, None] == np.arange(index.size)[None, :], BF16)


def peers(side, start):
    order = [
        (start[0] + i) % side * side + (start[1] + j) % side for i in range(side) for j in range(side)
    ]
    return order, np.argsort(order)


def orders(groups):
    side = int(round(groups**0.5))
    size = groups * LINE
    first, first_place = peers(side, FIRST)
    _, second_place = peers(side, SECOND)
    row = np.arange(size)
    half, place = row // (size // 2), row % (size // 2)
    block, inner = place // 4, place % 4
    natural = first_place[block] * LINE + half * 4 + inner
    turned = first_place[block % side * side + block // side] * LINE + half * 4 + inner
    spread = second_place[block] * LINE + half * 4 + inner
    part, func = row // groups, row % groups
    flat = second_place[np.asarray(first)[func]] * LINE + part % 2 * 4 + part // 2
    return natural, turned, spread, flat


def first_kernel(tile_ref, green_ref, m_ref, shard_ref, out_ref):
    tile, mu_tile = lax.axis_index("row") // 2, lax.axis_index("col") // 4
    green_tile = lax.axis_index("row") // 4
    length = m_ref.shape[1]

    def halves(count, low, high):
        line = lax.broadcasted_iota(jnp.int32, (count, TILE), 0) % LINE
        return jnp.where(line < 4, low.astype(F32), high.astype(F32))

    keep = halves(length, tile_ref[mu_tile, 0, tile], tile_ref[mu_tile, 1, tile])
    for k in range(out_ref.shape[0]):
        out_ref[k, :length] = (m_ref[k ^ ROWS].astype(F32) * keep).astype(BF16)
    keep_green = jnp.concatenate(
        [halves(LINE, green_ref[w, green_tile, 0], green_ref[w, green_tile, 1]) for w in range(2)], axis=0
    )
    shard = (shard_ref[...].astype(F32) * keep_green).astype(BF16)
    for k in range(out_ref.shape[0]):
        out_ref[k, length:] = shard


def second_kernel(got_ref, out_ref):
    rows = got_ref.shape[0]
    groups = out_ref.shape[0]
    length = groups // rows * LINE
    each = groups // rows
    for k in range(rows):
        out_ref[k * each : (k + 1) * each, :LINE] = got_ref[k ^ ROWS, :length].reshape(each, LINE, TILE)
    shard = got_ref[lax.axis_index("rep") ^ ROWS, length:]
    out_ref[:, LINE:] = jnp.broadcast_to(shard[None], (groups,) + shard.shape)


def product_kernel(natural_ref, turned_ref, spread_ref, got_ref, out_ref):
    groups = got_ref.shape[0]
    size = groups * LINE
    side = size // 2
    got = got_ref[...]
    m_part = got[:, :LINE].reshape(size, TILE)
    o_part = got[:, LINE : 2 * LINE].reshape(size, TILE)
    v_part = got[:, 2 * LINE :].reshape(size, TILE)
    natural = natural_ref[...]
    turned = turned_ref[...]

    def square(rows):
        rows = rows.astype(BF16)
        return jnp.concatenate([rows[:side], rows[side:]], axis=1)

    virtual = square(dot(turned, v_part))
    mine = square(dot(natural, m_part))
    occupied = square(dot(turned, o_part))
    halfway = dot(mine, virtual).astype(BF16)
    spread = spread_ref[...]
    wide = dot(occupied, spread[:side] + spread[side:]).astype(BF16)
    product = dot(wide, halfway, TN)
    line = lax.broadcasted_iota(jnp.int32, (size, TILE), 0) % LINE
    out = jnp.where(line < 4, product[:, :TILE], product[:, TILE:]).astype(BF16)
    out_ref[...] = out.reshape(groups, LINE, TILE)


def pair_kernel(order_ref, y_ref, held_ref, out_ref):
    count = y_ref.shape[0]
    half = count // 2
    picked = dot(order_ref[...], y_ref[...].reshape(count * LINE, TILE)).astype(BF16)
    flat = jnp.concatenate([picked[b * count : (b + 1) * count] for b in range(LINE)], axis=1)
    chip, core = lax.axis_index("row") // 2, lax.axis_index("row") % 2
    part = dot(held_ref[...], flat, NT)
    for step in range(4):
        for other in range(2):
            rows = part[(step * 2 + other) * count :][:count]
            wide = jnp.concatenate([rows[:half], rows[half:]], axis=1)
            block = lax.rem(chip - step + 4, 4) * 2 + lax.rem(core + other, 2)
            block = lax.rem(block + 8 - THIRD[0], 8)
            cut = THIRD[1] * 4
            wide = jnp.concatenate([wide[cut:], wide[:cut]], axis=0)
            out_ref[pl.ds(pl.multiple_of(block * half, half), half), :] = wide


def gather_kernel(*refs):
    count = refs[0].shape[0]
    for step, ref in enumerate(refs[:-1]):
        refs[-1][step * count : (step + 1) * count] = ref[...]


def cost(flops):
    return pl.CostEstimate(flops=flops, bytes_accessed=0, transcendentals=0)


def sum_kernel(got_ref, out_ref):
    size = got_ref.shape[0]
    total = jnp.sum(got_ref[...].reshape(size // 8, 8, TILE), axis=0)
    total = total[:4] + total[4:]
    out_ref[...] = jnp.concatenate([total[:, :64], total[:, 64:]], axis=0)


def exchange(array, start):
    order, _ = peers(lax.axis_size("col"), start)
    return lax.all_to_all(array, GRID, 0, 0, tiled=True, axis_index_groups=[order])


def body(m_tensor, green, tile_mask, green_mask):
    row_count, mu_block, ao_count = m_tensor.shape
    groups = lax.axis_size(GRID)
    rows = lax.axis_size("row")
    halves = ao_count // TILE
    line = halves * mu_block
    row = lax.axis_index("row")
    natural, turned, spread, flat_order = (pick(order) for order in orders(groups))

    own = m_tensor.reshape(row_count, mu_block, halves, TILE).transpose(0, 2, 1, 3)
    own = own.reshape(rows, row_count // rows * line, TILE)
    green_own = green.reshape(2, mu_block, halves, TILE).transpose(0, 2, 1, 3)
    green_own = green_own.reshape(2 * line, TILE)
    first = pl.pallas_call(
        first_kernel,
        out_shape=pltpu.VMEM((rows, row_count // rows * line + 2 * line, TILE), BF16),
        in_specs=[SMEM, SMEM, VMEM, VMEM],
        out_specs=VMEM,
    )(tile_mask.transpose(1, 2, 0), green_mask, own, green_own)
    order = [[k ^ ROWS for k in range(rows)]]
    first = lax.all_to_all(first, "row", 0, 0, tiled=True, axis_index_groups=order)
    sent = pl.pallas_call(
        second_kernel,
        out_shape=pltpu.VMEM((groups, 3 * line, TILE), BF16),
        in_specs=[VMEM],
        out_specs=VMEM,
    )(held(first))

    mu_tile = lax.axis_index(GRID) * mu_block // TILE
    keep_own = jnp.repeat(tile_mask[row * row_count // TILE, mu_tile].astype(BF16), TILE)
    right = m_tensor * keep_own[None, None, :]
    right = right.reshape(rows, 2, row_count // rows // 2, mu_block * ao_count).transpose(1, 0, 2, 3)
    right = right.reshape(row_count, mu_block * ao_count)

    def gathered(parts, flops):
        return pl.pallas_call(
            gather_kernel,
            out_shape=pltpu.VMEM((sum(part.shape[0] for part in parts), parts[0].shape[1]), BF16),
            in_specs=[VMEM] * len(parts),
            out_specs=VMEM,
            cost_estimate=cost(flops),
        )(*[held(part) for part in parts])

    other = lax.ppermute(right, "row", [(r, r ^ 1) for r in range(rows)])
    pair = gathered([right, other], COST_G)
    along = [lax.ppermute(pair, "row", [(r, (r + 2 * step) % rows) for r in range(rows)]) for step in (1, 2, 3)]
    near = gathered([pair] + along, COST_F)
    got = exchange(sent, FIRST)
    product = pl.pallas_call(
        product_kernel,
        out_shape=pltpu.VMEM((groups, line, TILE), BF16),
        in_specs=[VMEM, VMEM, VMEM, VMEM],
        out_specs=VMEM,
        cost_estimate=cost(COST_1),
    )(held(natural), held(turned), held(spread), held(got))
    contracted = exchange(product, SECOND)
    partial = pl.pallas_call(
        pair_kernel,
        out_shape=pltpu.VMEM((groups * 4, TILE), F32),
        in_specs=[VMEM, VMEM, VMEM],
        out_specs=VMEM,
        cost_estimate=cost(COST_A),
    )(held(flat_order), held(contracted), held(near))
    slices = exchange(partial.reshape(groups, 4, TILE), THIRD)
    result = pl.pallas_call(
        sum_kernel,
        out_shape=jax.ShapeDtypeStruct((8, row_count), F32),
        in_specs=[VMEM],
        out_specs=VMEM,
    )(held(slices.reshape(groups * 4, TILE)))
    return result.T


def solution(mesh):
    return jax.shard_map(
        body,
        mesh=mesh,
        in_specs=(P("row", ("col", "rep"), None), P(None, ("row", "col"), None), P(), P()),
        out_specs=P("row", ("col", "rep")),
        check_vma=False,
    )
```

```python
import jax
import jax.numpy as jnp
import numpy as np
from jax import lax
from jax.experimental import pallas as pl
from jax.experimental.pallas import tpu as pltpu
from jax.sharding import PartitionSpec as P

TILE = 128
START = 4
ROWS = 1
COST_F = 10**10
COST_A = 10**9
COST_1 = 1
COST_G = 10**10
GRID = ("col", "rep")
LINE = 8
BF16 = jnp.bfloat16
F32 = jnp.float32
VMEM = pl.BlockSpec(memory_space=pltpu.VMEM)
SMEM = pl.BlockSpec(memory_space=pltpu.SMEM)
NN = (((1,), (0,)), ((), ()))
NT = (((1,), (1,)), ((), ()))
TN = (((0,), (0,)), ((), ()))


def held(array):
    return pltpu.with_memory_space_constraint(array, pltpu.VMEM)


def dot(left, right, dims=NN):
    return lax.dot_general(left, right, dims, preferred_element_type=F32)


def pick(index):
    index = np.asarray(index)
    return jnp.asarray(index[:, None] == np.arange(index.size)[None, :], BF16)


def peers(side):
    order = [
        (START + i) % side * side + (START + j) % side for i in range(side) for j in range(side)
    ]
    return order, np.argsort(order)


def orders(groups):
    side = int(round(groups**0.5))
    size = groups * LINE
    order, place = peers(side)
    row = np.arange(size)
    half, nu = row // (size // 2), row % (size // 2)
    block, inner = nu // 4, nu % 4
    source = place[block % side * side + block // side]
    column = np.arange(size // 2)
    return source * LINE + half * 4 + inner, np.asarray(order)[column % groups] * 4 + column // groups


def first_kernel(tile_ref, green_ref, m_ref, shard_ref, out_ref):
    tile, mu_tile = lax.axis_index("row") // 2, lax.axis_index("col") // 4
    green_tile = lax.axis_index("row") // 4
    length = m_ref.shape[1]

    def halves(count, low, high):
        line = lax.broadcasted_iota(jnp.int32, (count, TILE), 0) % LINE
        return jnp.where(line < 4, low.astype(F32), high.astype(F32))

    keep = halves(length, tile_ref[mu_tile, 0, tile], tile_ref[mu_tile, 1, tile])
    for k in range(out_ref.shape[0]):
        out_ref[k, :length] = (m_ref[k ^ ROWS].astype(F32) * keep).astype(BF16)
    keep_green = jnp.concatenate(
        [halves(LINE, green_ref[w, green_tile, 0], green_ref[w, green_tile, 1]) for w in range(2)], axis=0
    )
    shard = (shard_ref[...].astype(F32) * keep_green).astype(BF16)
    for k in range(out_ref.shape[0]):
        out_ref[k, length:] = shard


def second_kernel(got_ref, out_ref):
    rows = got_ref.shape[0]
    groups = out_ref.shape[0]
    length = groups // rows * LINE
    each = groups // rows
    for k in range(rows):
        out_ref[k * each : (k + 1) * each, :LINE] = got_ref[k ^ ROWS, :length].reshape(each, LINE, TILE)
    shard = got_ref[lax.axis_index("rep") ^ ROWS, length:]
    out_ref[:, LINE:] = jnp.broadcast_to(shard[None], (groups,) + shard.shape)


def product_kernel(nu_ref, l_ref, got_ref, out_ref, m_ref, o_ref, y_ref):
    groups = got_ref.shape[0]
    side = 8
    size = groups * LINE
    got = got_ref[...]
    rows = dot(nu_ref[...], got[:, 2 * LINE :].reshape(size, TILE)).astype(BF16)
    virtual = jnp.concatenate([rows[: size // 2], rows[size // 2 :]], axis=1)
    m_ref[...] = got[:, :LINE].reshape(size, TILE).astype(F32)
    o_ref[...] = got[:, LINE : 2 * LINE].reshape(size, TILE).astype(F32)
    mine = [
        jnp.concatenate([m_ref[pl.ds(half * 4 + i, groups, stride=LINE), :] for i in range(4)], axis=0)
        for half in range(2)
    ]
    occupied = [
        jnp.concatenate(
            [
                o_ref[pl.ds(m * LINE + half * 4 + i, side, stride=side * LINE), :]
                for i in range(4)
                for m in range(side)
            ],
            axis=0,
        )
        for half in range(2)
    ]
    mine = jnp.concatenate(mine, axis=1).astype(BF16)
    occupied = jnp.concatenate(occupied, axis=1).astype(BF16)
    halfway = dot(mine, virtual).astype(BF16)
    product = dot(dot(occupied, l_ref[...]).astype(BF16), halfway, TN)
    for i in range(4):
        for half in range(2):
            block = product[i * groups : (i + 1) * groups, half * TILE : (half + 1) * TILE]
            y_ref[pl.ds(half * 4 + i, groups, stride=LINE), :] = block
    out_ref[...] = y_ref[...].astype(BF16).reshape(groups, LINE, TILE)


def pair_kernel(y_ref, *refs):
    out_ref, wide_ref = refs[-2:]
    count = y_ref.shape[0]
    half = count // 2
    wide_ref[...] = y_ref[...].reshape(count * LINE, TILE).astype(F32)
    picked = [wide_ref[pl.ds(line, count, stride=LINE), :].astype(BF16) for line in (0, 4, 1, 5, 2, 6, 3, 7)]
    flat = jnp.concatenate(picked, axis=1)
    chip, core = lax.axis_index("row") // 2, lax.axis_index("row") % 2
    for step in range(4):
        part = dot(refs[step][...], flat, NT)
        for other in range(2):
            rows = part[other * count :][:count]
            wide = jnp.concatenate([rows[:half], rows[half:]], axis=1)
            block = lax.rem(chip - step + 4, 4) * 2 + lax.rem(core + other, 2)
            block = lax.rem(block + 8 - START, 8)
            cut = START * 4
            wide = jnp.concatenate([wide[cut:], wide[:cut]], axis=0)
            out_ref[pl.ds(pl.multiple_of(block * half, half), half), :] = wide


def gather_kernel(*refs):
    count = refs[0].shape[0]
    for step, ref in enumerate(refs[:-1]):
        refs[-1][step * count : (step + 1) * count] = ref[...]


def cost(flops):
    return pl.CostEstimate(flops=flops, bytes_accessed=0, transcendentals=0)


def sum_kernel(got_ref, out_ref):
    size = got_ref.shape[0]
    total = jnp.sum(got_ref[...].reshape(size // 8, 8, TILE), axis=0)
    total = total[:4] + total[4:]
    out_ref[...] = jnp.concatenate([total[:, :64], total[:, 64:]], axis=0)


def exchange(array):
    order, _ = peers(lax.axis_size("col"))
    return lax.all_to_all(array, GRID, 0, 0, tiled=True, axis_index_groups=[order])


def body(m_tensor, green, tile_mask, green_mask):
    row_count, mu_block, ao_count = m_tensor.shape
    groups = lax.axis_size(GRID)
    rows = lax.axis_size("row")
    halves = ao_count // TILE
    line = halves * mu_block
    row = lax.axis_index("row")
    nu_order, l_order = orders(groups)

    own = m_tensor.reshape(row_count, mu_block, halves, TILE).transpose(0, 2, 1, 3)
    own = own.reshape(rows, row_count // rows * line, TILE)
    green_own = green.reshape(2, mu_block, halves, TILE).transpose(0, 2, 1, 3)
    green_own = green_own.reshape(2 * line, TILE)
    first = pl.pallas_call(
        first_kernel,
        out_shape=pltpu.VMEM((rows, row_count // rows * line + 2 * line, TILE), BF16),
        in_specs=[SMEM, SMEM, VMEM, VMEM],
        out_specs=VMEM,
    )(tile_mask.transpose(1, 2, 0), green_mask, own, green_own)
    order = [[k ^ ROWS for k in range(rows)]]
    first = lax.all_to_all(first, "row", 0, 0, tiled=True, axis_index_groups=order)
    sent = pl.pallas_call(
        second_kernel,
        out_shape=pltpu.VMEM((groups, 3 * line, TILE), BF16),
        in_specs=[VMEM],
        out_specs=VMEM,
    )(held(first))

    mu_tile = lax.axis_index(GRID) * mu_block // TILE
    keep_own = jnp.repeat(tile_mask[row * row_count // TILE, mu_tile].astype(BF16), TILE)
    right = m_tensor * keep_own[None, None, :]
    right = right.reshape(rows, 2, row_count // rows // 2, mu_block * ao_count).transpose(1, 0, 2, 3)
    right = right.reshape(row_count, mu_block * ao_count)

    def gathered(parts, flops):
        return pl.pallas_call(
            gather_kernel,
            out_shape=pltpu.VMEM((sum(part.shape[0] for part in parts), parts[0].shape[1]), BF16),
            in_specs=[VMEM] * len(parts),
            out_specs=VMEM,
            cost_estimate=cost(flops),
        )(*[held(part) for part in parts])

    other = lax.ppermute(right, "row", [(r, r ^ 1) for r in range(rows)])
    pair = gathered([right, other], COST_G)
    along = [lax.ppermute(pair, "row", [(r, (r + 2 * step) % rows) for r in range(rows)]) for step in (1, 2, 3)]
    got = exchange(sent)
    product = pl.pallas_call(
        product_kernel,
        out_shape=pltpu.VMEM((groups, line, TILE), BF16),
        in_specs=[VMEM, VMEM, VMEM],
        out_specs=VMEM,
        scratch_shapes=[pltpu.VMEM((groups * line, TILE), F32)] * 3,
        cost_estimate=cost(COST_1),
    )(held(pick(nu_order)), held(pick(l_order).T), held(got))
    contracted = exchange(product)
    partial = pl.pallas_call(
        pair_kernel,
        out_shape=pltpu.VMEM((groups * 4, TILE), F32),
        in_specs=[VMEM] * 5,
        out_specs=VMEM,
        scratch_shapes=[pltpu.VMEM((groups * line, TILE), F32)],
        cost_estimate=cost(COST_A),
    )(held(contracted), *[held(part) for part in [pair] + along])
    slices = exchange(partial.reshape(groups, 4, TILE))
    result = pl.pallas_call(
        sum_kernel,
        out_shape=jax.ShapeDtypeStruct((8, row_count), F32),
        in_specs=[VMEM],
        out_specs=VMEM,
    )(held(slices.reshape(groups * 4, TILE)))
    return result.T


def solution(mesh):
    return jax.shard_map(
        body,
        mesh=mesh,
        in_specs=(P("row", ("col", "rep"), None), P(None, ("row", "col"), None), P(), P()),
        out_specs=P("row", ("col", "rep")),
        check_vma=False,
    )
```

```python
import jax
import jax.numpy as jnp
import numpy as np
from jax import lax
from jax.experimental import pallas as pl
from jax.experimental.pallas import tpu as pltpu
from jax.sharding import PartitionSpec as P

TILE = 128
START = 4
ROWS = 1
COST_F = 1
COST_A = 1
COST_1 = 1
COST_G = 10**10
GRID = ("col", "rep")
LINE = 8
BF16 = jnp.bfloat16
F32 = jnp.float32
VMEM = pl.BlockSpec(memory_space=pltpu.VMEM)
SMEM = pl.BlockSpec(memory_space=pltpu.SMEM)
NN = (((1,), (0,)), ((), ()))
NT = (((1,), (1,)), ((), ()))
TN = (((0,), (0,)), ((), ()))


def held(array):
    return pltpu.with_memory_space_constraint(array, pltpu.VMEM)


def dot(left, right, dims=NN):
    return lax.dot_general(left, right, dims, preferred_element_type=F32)


def pick(index):
    index = np.asarray(index)
    return jnp.asarray(index[:, None] == np.arange(index.size)[None, :], BF16)


def peers(side):
    order = [
        (START + i) % side * side + (START + j) % side for i in range(side) for j in range(side)
    ]
    return order, np.argsort(order)


def orders(groups):
    side = int(round(groups**0.5))
    size = groups * LINE
    order, place = peers(side)
    row = np.arange(size)
    half, nu = row // (size // 2), row % (size // 2)
    block, inner = nu // 4, nu % 4
    source = place[block % side * side + block // side]
    column = np.arange(size // 2)
    return source * LINE + half * 4 + inner, np.asarray(order)[column % groups] * 4 + column // groups


def first_kernel(tile_ref, green_ref, m_ref, shard_ref, out_ref):
    tile, mu_tile = lax.axis_index("row") // 2, lax.axis_index("col") // 4
    green_tile = lax.axis_index("row") // 4
    length = m_ref.shape[1]

    def halves(count, low, high):
        line = lax.broadcasted_iota(jnp.int32, (count, TILE), 0) % LINE
        return jnp.where(line < 4, low.astype(F32), high.astype(F32))

    keep = halves(length, tile_ref[mu_tile, 0, tile], tile_ref[mu_tile, 1, tile])
    for k in range(out_ref.shape[0]):
        out_ref[k, :length] = (m_ref[k ^ ROWS].astype(F32) * keep).astype(BF16)
    keep_green = jnp.concatenate(
        [halves(LINE, green_ref[w, green_tile, 0], green_ref[w, green_tile, 1]) for w in range(2)], axis=0
    )
    shard = (shard_ref[...].astype(F32) * keep_green).astype(BF16)
    for k in range(out_ref.shape[0]):
        out_ref[k, length:] = shard


def second_kernel(got_ref, out_ref):
    rows = got_ref.shape[0]
    groups = out_ref.shape[0]
    length = groups // rows * LINE
    each = groups // rows
    for k in range(rows):
        out_ref[k * each : (k + 1) * each, :LINE] = got_ref[k ^ ROWS, :length].reshape(each, LINE, TILE)
    shard = got_ref[lax.axis_index("rep") ^ ROWS, length:]
    out_ref[:, LINE:] = jnp.broadcast_to(shard[None], (groups,) + shard.shape)


def product_kernel(nu_ref, l_ref, got_ref, out_ref, m_ref, o_ref, y_ref):
    groups = got_ref.shape[0]
    side = 8
    size = groups * LINE
    got = got_ref[...]
    rows = dot(nu_ref[...], got[:, 2 * LINE :].reshape(size, TILE)).astype(BF16)
    virtual = jnp.concatenate([rows[: size // 2], rows[size // 2 :]], axis=1)
    m_ref[...] = got[:, :LINE].reshape(size, TILE).astype(F32)
    o_ref[...] = got[:, LINE : 2 * LINE].reshape(size, TILE).astype(F32)
    mine = [
        jnp.concatenate([m_ref[pl.ds(half * 4 + i, groups, stride=LINE), :] for i in range(4)], axis=0)
        for half in range(2)
    ]
    occupied = [
        jnp.concatenate(
            [
                o_ref[pl.ds(m * LINE + half * 4 + i, side, stride=side * LINE), :]
                for i in range(4)
                for m in range(side)
            ],
            axis=0,
        )
        for half in range(2)
    ]
    mine = jnp.concatenate(mine, axis=1).astype(BF16)
    occupied = jnp.concatenate(occupied, axis=1).astype(BF16)
    halfway = dot(mine, virtual).astype(BF16)
    product = dot(dot(occupied, l_ref[...]).astype(BF16), halfway, TN)
    for i in range(4):
        for half in range(2):
            block = product[i * groups : (i + 1) * groups, half * TILE : (half + 1) * TILE]
            y_ref[pl.ds(half * 4 + i, groups, stride=LINE), :] = block
    out_ref[...] = y_ref[...].astype(BF16).reshape(groups, LINE, TILE)


def near_kernel(y_ref, pair_ref, out_ref, flat_ref, wide_ref):
    count = y_ref.shape[0]
    wide_ref[...] = y_ref[...].reshape(count * LINE, TILE).astype(F32)
    picked = [wide_ref[pl.ds(line, count, stride=LINE), :].astype(BF16) for line in (0, 4, 1, 5, 2, 6, 3, 7)]
    flat = jnp.concatenate(picked, axis=1)
    flat_ref[...] = flat
    place(flat, pair_ref, 0, out_ref)


def far_kernel(flat_ref, part_ref, *refs):
    out_ref = refs[-1]
    out_ref[...] = part_ref[...]
    for step, ref in enumerate(refs[:-1]):
        place(flat_ref[...], ref, step + 1, out_ref)


def place(flat, pair_ref, step, out_ref):
    count = flat.shape[0]
    half = count // 2
    chip, core = lax.axis_index("row") // 2, lax.axis_index("row") % 2
    part = dot(pair_ref[...], flat, NT)
    for other in range(2):
        rows = part[other * count :][:count]
        wide = jnp.concatenate([rows[:half], rows[half:]], axis=1)
        block = lax.rem(chip - step + 4, 4) * 2 + lax.rem(core + other, 2)
        block = lax.rem(block + 8 - START, 8)
        cut = START * 4
        wide = jnp.concatenate([wide[cut:], wide[:cut]], axis=0)
        out_ref[pl.ds(pl.multiple_of(block * half, half), half), :] = wide


def gather_kernel(*refs):
    count = refs[0].shape[0]
    for step, ref in enumerate(refs[:-1]):
        refs[-1][step * count : (step + 1) * count] = ref[...]


def cost(flops):
    return pl.CostEstimate(flops=flops, bytes_accessed=0, transcendentals=0)


def sum_kernel(got_ref, out_ref):
    size = got_ref.shape[0]
    total = jnp.sum(got_ref[...].reshape(size // 8, 8, TILE), axis=0)
    total = total[:4] + total[4:]
    out_ref[...] = jnp.concatenate([total[:, :64], total[:, 64:]], axis=0)


def exchange(array):
    order, _ = peers(lax.axis_size("col"))
    return lax.all_to_all(array, GRID, 0, 0, tiled=True, axis_index_groups=[order])


def body(m_tensor, green, tile_mask, green_mask):
    row_count, mu_block, ao_count = m_tensor.shape
    groups = lax.axis_size(GRID)
    rows = lax.axis_size("row")
    halves = ao_count // TILE
    line = halves * mu_block
    row = lax.axis_index("row")
    nu_order, l_order = orders(groups)

    own = m_tensor.reshape(row_count, mu_block, halves, TILE).transpose(0, 2, 1, 3)
    own = own.reshape(rows, row_count // rows * line, TILE)
    green_own = green.reshape(2, mu_block, halves, TILE).transpose(0, 2, 1, 3)
    green_own = green_own.reshape(2 * line, TILE)
    first = pl.pallas_call(
        first_kernel,
        out_shape=pltpu.VMEM((rows, row_count // rows * line + 2 * line, TILE), BF16),
        in_specs=[SMEM, SMEM, VMEM, VMEM],
        out_specs=VMEM,
    )(tile_mask.transpose(1, 2, 0), green_mask, own, green_own)
    order = [[k ^ ROWS for k in range(rows)]]
    first = lax.all_to_all(first, "row", 0, 0, tiled=True, axis_index_groups=order)
    sent = pl.pallas_call(
        second_kernel,
        out_shape=pltpu.VMEM((groups, 3 * line, TILE), BF16),
        in_specs=[VMEM],
        out_specs=VMEM,
    )(held(first))

    mu_tile = lax.axis_index(GRID) * mu_block // TILE
    keep_own = jnp.repeat(tile_mask[row * row_count // TILE, mu_tile].astype(BF16), TILE)
    right = m_tensor * keep_own[None, None, :]
    right = right.reshape(rows, 2, row_count // rows // 2, mu_block * ao_count).transpose(1, 0, 2, 3)
    right = right.reshape(row_count, mu_block * ao_count)

    def gathered(parts, flops):
        return pl.pallas_call(
            gather_kernel,
            out_shape=pltpu.VMEM((sum(part.shape[0] for part in parts), parts[0].shape[1]), BF16),
            in_specs=[VMEM] * len(parts),
            out_specs=VMEM,
            cost_estimate=cost(flops),
        )(*[held(part) for part in parts])

    other = lax.ppermute(right, "row", [(r, r ^ 1) for r in range(rows)])
    pair = gathered([right, other], COST_G)
    along = [lax.ppermute(pair, "row", [(r, (r + 2 * step) % rows) for r in range(rows)]) for step in (1, 2, 3)]
    got = exchange(sent)
    product = pl.pallas_call(
        product_kernel,
        out_shape=pltpu.VMEM((groups, line, TILE), BF16),
        in_specs=[VMEM, VMEM, VMEM],
        out_specs=VMEM,
        scratch_shapes=[pltpu.VMEM((groups * line, TILE), F32)] * 3,
        cost_estimate=cost(COST_1),
    )(held(pick(nu_order)), held(pick(l_order).T), held(got))
    contracted = exchange(product)
    partial, flat = pl.pallas_call(
        near_kernel,
        out_shape=(
            pltpu.VMEM((groups * 4, TILE), F32),
            pltpu.VMEM((row_count, mu_block * ao_count), BF16),
        ),
        in_specs=[VMEM] * 2,
        out_specs=(VMEM, VMEM),
        scratch_shapes=[pltpu.VMEM((groups * line, TILE), F32)],
        cost_estimate=cost(COST_A),
    )(held(contracted), held(pair))
    partial = pl.pallas_call(
        far_kernel,
        out_shape=pltpu.VMEM((groups * 4, TILE), F32),
        in_specs=[VMEM] * 5,
        out_specs=VMEM,
        cost_estimate=cost(COST_F),
    )(held(flat), held(partial), *[held(part) for part in along])
    slices = exchange(partial.reshape(groups, 4, TILE))
    result = pl.pallas_call(
        sum_kernel,
        out_shape=jax.ShapeDtypeStruct((8, row_count), F32),
        in_specs=[VMEM],
        out_specs=VMEM,
    )(held(slices.reshape(groups * 4, TILE)))
    return result.T


def solution(mesh):
    return jax.shard_map(
        body,
        mesh=mesh,
        in_specs=(P("row", ("col", "rep"), None), P(None, ("row", "col"), None), P(), P()),
        out_specs=P("row", ("col", "rep")),
        check_vma=False,
    )
```

```python
import jax
import jax.numpy as jnp
import numpy as np
from jax import lax
from jax.experimental import pallas as pl
from jax.experimental.pallas import tpu as pltpu
from jax.sharding import PartitionSpec as P

TILE = 128
START = 4
ROWS = 5
COST_F = 1
COST_A = 1
COST_1 = 1
COST_G = 10**10
COST_H = 1
GRID = ("col", "rep")
LINE = 8
BF16 = jnp.bfloat16
F32 = jnp.float32
VMEM = pl.BlockSpec(memory_space=pltpu.VMEM)
SMEM = pl.BlockSpec(memory_space=pltpu.SMEM)
NN = (((1,), (0,)), ((), ()))
NT = (((1,), (1,)), ((), ()))
TN = (((0,), (0,)), ((), ()))


def held(array):
    return pltpu.with_memory_space_constraint(array, pltpu.VMEM)


def dot(left, right, dims=NN):
    return lax.dot_general(left, right, dims, preferred_element_type=F32)


def pick(index):
    index = np.asarray(index)
    return jnp.asarray(index[:, None] == np.arange(index.size)[None, :], BF16)


def peers(side):
    order = [
        (START + i) % side * side + (START + j) % side for i in range(side) for j in range(side)
    ]
    return order, np.argsort(order)


def orders(groups):
    side = int(round(groups**0.5))
    size = groups * LINE
    order, place = peers(side)
    row = np.arange(size)
    half, nu = row // (size // 2), row % (size // 2)
    block, inner = nu // 4, nu % 4
    source = place[block % side * side + block // side]
    column = np.arange(size // 2)
    return source * LINE + half * 4 + inner, np.asarray(order)[column % groups] * 4 + column // groups


def first_kernel(tile_ref, green_ref, m_ref, shard_ref, out_ref):
    tile, mu_tile = lax.axis_index("row") // 2, lax.axis_index("col") // 4
    green_tile = lax.axis_index("row") // 4
    length = m_ref.shape[1]

    def halves(count, low, high):
        line = lax.broadcasted_iota(jnp.int32, (count, TILE), 0) % LINE
        return jnp.where(line < 4, low.astype(F32), high.astype(F32))

    keep = halves(length, tile_ref[mu_tile, 0, tile], tile_ref[mu_tile, 1, tile])
    for k in range(out_ref.shape[0]):
        out_ref[k, :length] = (m_ref[k ^ ROWS].astype(F32) * keep).astype(BF16)
    keep_green = jnp.concatenate(
        [halves(LINE, green_ref[w, green_tile, 0], green_ref[w, green_tile, 1]) for w in range(2)], axis=0
    )
    shard = (shard_ref[...].astype(F32) * keep_green).astype(BF16)
    for k in range(out_ref.shape[0]):
        out_ref[k, length:] = shard


def second_kernel(got_ref, out_ref):
    rows = got_ref.shape[0]
    groups = out_ref.shape[0]
    length = groups // rows * LINE
    each = groups // rows
    for k in range(rows):
        out_ref[k * each : (k + 1) * each, :LINE] = got_ref[k ^ ROWS, :length].reshape(each, LINE, TILE)
    shard = got_ref[lax.axis_index("rep") ^ ROWS, length:]
    out_ref[:, LINE:] = jnp.broadcast_to(shard[None], (groups,) + shard.shape)


def product_kernel(nu_ref, l_ref, got_ref, out_ref, m_ref, o_ref, y_ref):
    groups = got_ref.shape[0]
    side = 8
    size = groups * LINE
    got = got_ref[...]
    rows = dot(nu_ref[...], got[:, 2 * LINE :].reshape(size, TILE)).astype(BF16)
    virtual = jnp.concatenate([rows[: size // 2], rows[size // 2 :]], axis=1)
    m_ref[...] = got[:, :LINE].reshape(size, TILE).astype(F32)
    o_ref[...] = got[:, LINE : 2 * LINE].reshape(size, TILE).astype(F32)
    mine = [
        jnp.concatenate([m_ref[pl.ds(half * 4 + i, groups, stride=LINE), :] for i in range(4)], axis=0)
        for half in range(2)
    ]
    occupied = [
        jnp.concatenate(
            [
                o_ref[pl.ds(m * LINE + half * 4 + i, side, stride=side * LINE), :]
                for i in range(4)
                for m in range(side)
            ],
            axis=0,
        )
        for half in range(2)
    ]
    mine = jnp.concatenate(mine, axis=1).astype(BF16)
    occupied = jnp.concatenate(occupied, axis=1).astype(BF16)
    halfway = dot(mine, virtual).astype(BF16)
    product = dot(dot(occupied, l_ref[...]).astype(BF16), halfway, TN)
    for i in range(4):
        for half in range(2):
            block = product[i * groups : (i + 1) * groups, half * TILE : (half + 1) * TILE]
            y_ref[pl.ds(half * 4 + i, groups, stride=LINE), :] = block
    out_ref[...] = y_ref[...].astype(BF16).reshape(groups, LINE, TILE)


def near_kernel(y_ref, near_ref, out_ref, flat_ref, wide_ref):
    count = y_ref.shape[0]
    wide_ref[...] = y_ref[...].reshape(count * LINE, TILE).astype(F32)
    picked = [wide_ref[pl.ds(line, count, stride=LINE), :].astype(BF16) for line in (0, 4, 1, 5, 2, 6, 3, 7)]
    flat = jnp.concatenate(picked, axis=1)
    flat_ref[...] = flat
    place(flat, near_ref, 0, out_ref)


def far_kernel(flat_ref, part_ref, far_ref, out_ref):
    out_ref[...] = part_ref[...]
    place(flat_ref[...], far_ref, 2, out_ref)


def place(flat, held_ref, base, out_ref):
    count = flat.shape[0]
    half = count // 2
    part = dot(held_ref[...], flat, NT)
    for index, mask in enumerate((0, 4, 1, 5)):
        rows = part[index * count :][:count]
        wide = jnp.concatenate([rows[:half], rows[half:]], axis=1)
        block = lax.rem((lax.axis_index("row") ^ (mask ^ base)) + 8 - START, 8)
        cut = START * 4
        wide = jnp.concatenate([wide[cut:], wide[:cut]], axis=0)
        out_ref[pl.ds(pl.multiple_of(block * half, half), half), :] = wide


def gather_kernel(*refs):
    count = refs[0].shape[0]
    for step, ref in enumerate(refs[:-1]):
        refs[-1][step * count : (step + 1) * count] = ref[...]


def cost(flops):
    return pl.CostEstimate(flops=flops, bytes_accessed=0, transcendentals=0)


def sum_kernel(got_ref, out_ref):
    size = got_ref.shape[0]
    total = jnp.sum(got_ref[...].reshape(size // 8, 8, TILE), axis=0)
    total = total[:4] + total[4:]
    out_ref[...] = jnp.concatenate([total[:, :64], total[:, 64:]], axis=0)


def exchange(array):
    order, _ = peers(lax.axis_size("col"))
    return lax.all_to_all(array, GRID, 0, 0, tiled=True, axis_index_groups=[order])


def body(m_tensor, green, tile_mask, green_mask):
    row_count, mu_block, ao_count = m_tensor.shape
    groups = lax.axis_size(GRID)
    rows = lax.axis_size("row")
    halves = ao_count // TILE
    line = halves * mu_block
    row = lax.axis_index("row")
    nu_order, l_order = orders(groups)

    own = m_tensor.reshape(row_count, mu_block, halves, TILE).transpose(0, 2, 1, 3)
    own = own.reshape(rows, row_count // rows * line, TILE)
    green_own = green.reshape(2, mu_block, halves, TILE).transpose(0, 2, 1, 3)
    green_own = green_own.reshape(2 * line, TILE)
    first = pl.pallas_call(
        first_kernel,
        out_shape=pltpu.VMEM((rows, row_count // rows * line + 2 * line, TILE), BF16),
        in_specs=[SMEM, SMEM, VMEM, VMEM],
        out_specs=VMEM,
    )(tile_mask.transpose(1, 2, 0), green_mask, own, green_own)
    order = [[k ^ ROWS for k in range(rows)]]
    first = lax.all_to_all(first, "row", 0, 0, tiled=True, axis_index_groups=order)
    sent = pl.pallas_call(
        second_kernel,
        out_shape=pltpu.VMEM((groups, 3 * line, TILE), BF16),
        in_specs=[VMEM],
        out_specs=VMEM,
    )(held(first))

    mu_tile = lax.axis_index(GRID) * mu_block // TILE
    keep_own = jnp.repeat(tile_mask[row * row_count // TILE, mu_tile].astype(BF16), TILE)
    right = m_tensor * keep_own[None, None, :]
    right = right.reshape(rows, 2, row_count // rows // 2, mu_block * ao_count).transpose(1, 0, 2, 3)
    right = right.reshape(row_count, mu_block * ao_count)

    def gathered(parts, flops):
        return pl.pallas_call(
            gather_kernel,
            out_shape=pltpu.VMEM((sum(part.shape[0] for part in parts), parts[0].shape[1]), BF16),
            in_specs=[VMEM] * len(parts),
            out_specs=VMEM,
            cost_estimate=cost(flops),
        )(*[held(part) for part in parts])

    def swap(array, bit):
        return lax.ppermute(array, "row", [(r, r ^ bit) for r in range(rows)])

    near = gathered([right, swap(right, 4)], COST_G)
    near = gathered([near, swap(near, 1)], COST_H)
    far = swap(near, 2)
    got = exchange(sent)
    product = pl.pallas_call(
        product_kernel,
        out_shape=pltpu.VMEM((groups, line, TILE), BF16),
        in_specs=[VMEM, VMEM, VMEM],
        out_specs=VMEM,
        scratch_shapes=[pltpu.VMEM((groups * line, TILE), F32)] * 3,
        cost_estimate=cost(COST_1),
    )(held(pick(nu_order)), held(pick(l_order).T), held(got))
    contracted = exchange(product)
    partial, flat = pl.pallas_call(
        near_kernel,
        out_shape=(
            pltpu.VMEM((groups * 4, TILE), F32),
            pltpu.VMEM((row_count, mu_block * ao_count), BF16),
        ),
        in_specs=[VMEM] * 2,
        out_specs=(VMEM, VMEM),
        scratch_shapes=[pltpu.VMEM((groups * line, TILE), F32)],
        cost_estimate=cost(COST_A),
    )(held(contracted), held(near))
    partial = pl.pallas_call(
        far_kernel,
        out_shape=pltpu.VMEM((groups * 4, TILE), F32),
        in_specs=[VMEM] * 3,
        out_specs=VMEM,
        cost_estimate=cost(COST_F),
    )(held(flat), held(partial), held(far))
    slices = exchange(partial.reshape(groups, 4, TILE))
    result = pl.pallas_call(
        sum_kernel,
        out_shape=jax.ShapeDtypeStruct((8, row_count), F32),
        in_specs=[VMEM],
        out_specs=VMEM,
    )(held(slices.reshape(groups * 4, TILE)))
    return result.T


def solution(mesh):
    return jax.shard_map(
        body,
        mesh=mesh,
        in_specs=(P("row", ("col", "rep"), None), P(None, ("row", "col"), None), P(), P()),
        out_specs=P("row", ("col", "rep")),
        check_vma=False,
    )
```

```python
import jax
import jax.numpy as jnp
import numpy as np
from jax import lax
from jax.experimental import pallas as pl
from jax.experimental.pallas import tpu as pltpu
from jax.sharding import PartitionSpec as P

TILE = 128
START = 4
ROWS = 5
COST_F = 1
COST_A = 1
COST_1 = 1
COST_G = 10**10
COST_H = 1
GRID = ("col", "rep")
LINE = 8
BF16 = jnp.bfloat16
F32 = jnp.float32
VMEM = pl.BlockSpec(memory_space=pltpu.VMEM)
SMEM = pl.BlockSpec(memory_space=pltpu.SMEM)
NN = (((1,), (0,)), ((), ()))
NT = (((1,), (1,)), ((), ()))
TN = (((0,), (0,)), ((), ()))


def held(array):
    return pltpu.with_memory_space_constraint(array, pltpu.VMEM)


def dot(left, right, dims=NN):
    return lax.dot_general(left, right, dims, preferred_element_type=F32)


def pick(index):
    index = np.asarray(index)
    return jnp.asarray(index[:, None] == np.arange(index.size)[None, :], BF16)


def peers(side):
    order = [
        (START + i) % side * side + (START + j) % side for i in range(side) for j in range(side)
    ]
    return order, np.argsort(order)


def orders(groups):
    side = int(round(groups**0.5))
    size = groups * LINE
    order, place = peers(side)
    row = np.arange(size)
    half, nu = row // (size // 2), row % (size // 2)
    block, inner = nu // 4, nu % 4
    source = place[block % side * side + block // side]
    column = np.arange(size // 2)
    return source * LINE + half * 4 + inner, np.asarray(order)[column % groups] * 4 + column // groups


def first_kernel(tile_ref, green_ref, m_ref, shard_ref, out_ref):
    tile, mu_tile = lax.axis_index("row") // 2, lax.axis_index("col") // 4
    green_tile = lax.axis_index("row") // 4
    length = m_ref.shape[1]

    def halves(count, low, high):
        line = lax.broadcasted_iota(jnp.int32, (count, TILE), 0) % LINE
        return jnp.where(line < 4, low.astype(F32), high.astype(F32))

    keep = halves(length, tile_ref[mu_tile, 0, tile], tile_ref[mu_tile, 1, tile])
    for k in range(out_ref.shape[0]):
        out_ref[k, :length] = (m_ref[k ^ ROWS].astype(F32) * keep).astype(BF16)
    keep_green = jnp.concatenate(
        [halves(LINE, green_ref[w, green_tile, 0], green_ref[w, green_tile, 1]) for w in range(2)], axis=0
    )
    shard = (shard_ref[...].astype(F32) * keep_green).astype(BF16)
    for k in range(out_ref.shape[0]):
        out_ref[k, length:] = shard


def second_kernel(got_ref, out_ref):
    rows = got_ref.shape[0]
    groups = out_ref.shape[0]
    length = groups // rows * LINE
    each = groups // rows
    for k in range(rows):
        out_ref[k * each : (k + 1) * each, :LINE] = got_ref[k ^ ROWS, :length].reshape(each, LINE, TILE)
    shard = got_ref[lax.axis_index("rep") ^ ROWS, length:]
    out_ref[:, LINE:] = jnp.broadcast_to(shard[None], (groups,) + shard.shape)


def product_kernel(nu_ref, l_ref, got_ref, out_ref, m_ref, o_ref, y_ref):
    groups = got_ref.shape[0]
    side = 8
    size = groups * LINE
    got = got_ref[...]
    rows = dot(nu_ref[...], got[:, 2 * LINE :].reshape(size, TILE)).astype(BF16)
    virtual = jnp.concatenate([rows[: size // 2], rows[size // 2 :]], axis=1)
    m_ref[:size] = got[:, :LINE].reshape(size, TILE).astype(F32)
    o_ref[:size] = got[:, LINE : 2 * LINE].reshape(size, TILE).astype(F32)
    mine = [
        jnp.concatenate([m_ref[pl.ds(half * 4 + i, groups, stride=LINE), :] for i in range(4)], axis=0)
        for half in range(2)
    ]
    occupied = [
        jnp.concatenate(
            [
                o_ref[pl.ds(m * LINE + half * 4 + i, side, stride=side * LINE), :]
                for i in range(4)
                for m in range(side)
            ],
            axis=0,
        )
        for half in range(2)
    ]
    mine = jnp.concatenate(mine, axis=1).astype(BF16)
    occupied = jnp.concatenate(occupied, axis=1).astype(BF16)
    halfway = dot(mine, virtual).astype(BF16)
    product = dot(dot(occupied, l_ref[...]).astype(BF16), halfway, TN)
    for i in range(4):
        for half in range(2):
            block = product[i * groups : (i + 1) * groups, half * TILE : (half + 1) * TILE]
            y_ref[pl.ds(half * 4 + i, groups, stride=LINE), :] = block
    out_ref[...] = y_ref[:size].astype(BF16).reshape(groups, LINE, TILE)


def near_kernel(y_ref, near_ref, out_ref, flat_ref, wide_ref):
    count = y_ref.shape[0]
    wide_ref[: count * LINE] = y_ref[...].reshape(count * LINE, TILE).astype(F32)
    picked = [wide_ref[pl.ds(line, count, stride=LINE), :].astype(BF16) for line in (0, 4, 1, 5, 2, 6, 3, 7)]
    flat = jnp.concatenate(picked, axis=1)
    flat_ref[...] = flat
    place(flat, near_ref, 0, out_ref)


def far_kernel(flat_ref, part_ref, far_ref, out_ref):
    out_ref[...] = part_ref[...]
    place(flat_ref[...], far_ref, 2, out_ref)


def place(flat, held_ref, base, out_ref):
    count = flat.shape[0]
    half = count // 2
    part = dot(held_ref[...], flat, NT)
    for index, mask in enumerate((0, 4, 1, 5)):
        rows = part[index * count :][:count]
        wide = jnp.concatenate([rows[:half], rows[half:]], axis=1)
        block = lax.rem((lax.axis_index("row") ^ (mask ^ base)) + 8 - START, 8)
        cut = START * 4
        wide = jnp.concatenate([wide[cut:], wide[:cut]], axis=0)
        out_ref[pl.ds(pl.multiple_of(block * half, half), half), :] = wide


def gather_kernel(*refs):
    count = refs[0].shape[0]
    for step, ref in enumerate(refs[:-1]):
        refs[-1][step * count : (step + 1) * count] = ref[...]


def cost(flops):
    return pl.CostEstimate(flops=flops, bytes_accessed=0, transcendentals=0)


def sum_kernel(got_ref, out_ref):
    size = got_ref.shape[0]
    total = jnp.sum(got_ref[...].reshape(size // 8, 8, TILE), axis=0)
    total = total[:4] + total[4:]
    out_ref[...] = jnp.concatenate([total[:, :64], total[:, 64:]], axis=0)


def exchange(array):
    order, _ = peers(lax.axis_size("col"))
    return lax.all_to_all(array, GRID, 0, 0, tiled=True, axis_index_groups=[order])


def body(m_tensor, green, tile_mask, green_mask):
    row_count, mu_block, ao_count = m_tensor.shape
    groups = lax.axis_size(GRID)
    rows = lax.axis_size("row")
    halves = ao_count // TILE
    line = halves * mu_block
    row = lax.axis_index("row")
    nu_order, l_order = orders(groups)

    own = m_tensor.reshape(row_count, mu_block, halves, TILE).transpose(0, 2, 1, 3)
    own = own.reshape(rows, row_count // rows * line, TILE)
    green_own = green.reshape(2, mu_block, halves, TILE).transpose(0, 2, 1, 3)
    green_own = green_own.reshape(2 * line, TILE)
    first = pl.pallas_call(
        first_kernel,
        out_shape=pltpu.VMEM((rows, row_count // rows * line + 2 * line, TILE), BF16),
        in_specs=[SMEM, SMEM, VMEM, VMEM],
        out_specs=VMEM,
    )(tile_mask.transpose(1, 2, 0), green_mask, own, green_own)
    order = [[k ^ ROWS for k in range(rows)]]
    first = lax.all_to_all(first, "row", 0, 0, tiled=True, axis_index_groups=order)
    sent = pl.pallas_call(
        second_kernel,
        out_shape=pltpu.VMEM((groups, 3 * line, TILE), BF16),
        in_specs=[VMEM],
        out_specs=VMEM,
    )(held(first))

    mu_tile = lax.axis_index(GRID) * mu_block // TILE
    keep_own = jnp.repeat(tile_mask[row * row_count // TILE, mu_tile].astype(BF16), TILE)
    right = m_tensor * keep_own[None, None, :]
    right = right.reshape(rows, 2, row_count // rows // 2, mu_block * ao_count).transpose(1, 0, 2, 3)
    right = right.reshape(row_count, mu_block * ao_count)

    def gathered(parts, flops):
        return pl.pallas_call(
            gather_kernel,
            out_shape=pltpu.VMEM((sum(part.shape[0] for part in parts), parts[0].shape[1]), BF16),
            in_specs=[VMEM] * len(parts),
            out_specs=VMEM,
            cost_estimate=cost(flops),
        )(*[held(part) for part in parts])

    def swap(array, bit):
        return lax.ppermute(array, "row", [(r, r ^ bit) for r in range(rows)])

    near = gathered([right, swap(right, 4)], COST_G)
    near = gathered([near, swap(near, 1)], COST_H)
    far = swap(near, 2)
    got = exchange(sent)
    product = pl.pallas_call(
        product_kernel,
        out_shape=pltpu.VMEM((groups, line, TILE), BF16),
        in_specs=[VMEM, VMEM, VMEM],
        out_specs=VMEM,
        scratch_shapes=[pltpu.VMEM((groups * line + rows * line, TILE), F32)] * 3,
        cost_estimate=cost(COST_1),
    )(held(pick(nu_order)), held(pick(l_order).T), held(got))
    contracted = exchange(product)
    partial, flat = pl.pallas_call(
        near_kernel,
        out_shape=(
            pltpu.VMEM((groups * 4, TILE), F32),
            pltpu.VMEM((row_count, mu_block * ao_count), BF16),
        ),
        in_specs=[VMEM] * 2,
        out_specs=(VMEM, VMEM),
        scratch_shapes=[pltpu.VMEM((groups * line + rows * line, TILE), F32)],
        cost_estimate=cost(COST_A),
    )(held(contracted), held(near))
    partial = pl.pallas_call(
        far_kernel,
        out_shape=pltpu.VMEM((groups * 4, TILE), F32),
        in_specs=[VMEM] * 3,
        out_specs=VMEM,
        cost_estimate=cost(COST_F),
    )(held(flat), held(partial), held(far))
    slices = exchange(partial.reshape(groups, 4, TILE))
    result = pl.pallas_call(
        sum_kernel,
        out_shape=jax.ShapeDtypeStruct((8, row_count), F32),
        in_specs=[VMEM],
        out_specs=VMEM,
    )(held(slices.reshape(groups * 4, TILE)))
    return result.T


def solution(mesh):
    return jax.shard_map(
        body,
        mesh=mesh,
        in_specs=(P("row", ("col", "rep"), None), P(None, ("row", "col"), None), P(), P()),
        out_specs=P("row", ("col", "rep")),
        check_vma=False,
    )
```

```python
import jax
import jax.numpy as jnp
import numpy as np
from jax import lax
from jax.experimental import pallas as pl
from jax.experimental.pallas import tpu as pltpu
from jax.sharding import PartitionSpec as P

TILE = 128
START = 4
ROWS = 5
COST_F = 1
COST_A = 1
COST_1 = 1
COST_G = 2 * 10**9
COST_H = 1
GRID = ("col", "rep")
LINE = 8
BF16 = jnp.bfloat16
F32 = jnp.float32
VMEM = pl.BlockSpec(memory_space=pltpu.VMEM)
SMEM = pl.BlockSpec(memory_space=pltpu.SMEM)
NN = (((1,), (0,)), ((), ()))
NT = (((1,), (1,)), ((), ()))
TN = (((0,), (0,)), ((), ()))


def held(array):
    return pltpu.with_memory_space_constraint(array, pltpu.VMEM)


def dot(left, right, dims=NN):
    return lax.dot_general(left, right, dims, preferred_element_type=F32)


def pick(index):
    index = np.asarray(index)
    return jnp.asarray(index[:, None] == np.arange(index.size)[None, :], BF16)


def peers(side):
    order = [
        (START + i) % side * side + (START + j) % side for i in range(side) for j in range(side)
    ]
    return order, np.argsort(order)


def orders(groups):
    side = int(round(groups**0.5))
    size = groups * LINE
    order, place = peers(side)
    row = np.arange(size)
    half, nu = row // (size // 2), row % (size // 2)
    block, inner = nu // 4, nu % 4
    source = place[block % side * side + block // side]
    column = np.arange(size // 2)
    return source * LINE + half * 4 + inner, np.asarray(order)[column % groups] * 4 + column // groups


def first_kernel(tile_ref, green_ref, m_ref, shard_ref, out_ref):
    tile, mu_tile = lax.axis_index("row") // 2, lax.axis_index("col") // 4
    green_tile = lax.axis_index("row") // 4
    length = m_ref.shape[1]

    def halves(count, low, high):
        line = lax.broadcasted_iota(jnp.int32, (count, TILE), 0) % LINE
        return jnp.where(line < 4, low.astype(F32), high.astype(F32))

    keep = halves(length, tile_ref[mu_tile, 0, tile], tile_ref[mu_tile, 1, tile])
    for k in range(out_ref.shape[0]):
        out_ref[k, :length] = (m_ref[k ^ ROWS].astype(F32) * keep).astype(BF16)
    keep_green = jnp.concatenate(
        [halves(LINE, green_ref[w, green_tile, 0], green_ref[w, green_tile, 1]) for w in range(2)], axis=0
    )
    shard = (shard_ref[...].astype(F32) * keep_green).astype(BF16)
    for k in range(out_ref.shape[0]):
        out_ref[k, length:] = shard


def second_kernel(got_ref, out_ref):
    rows = got_ref.shape[0]
    groups = out_ref.shape[0]
    length = groups // rows * LINE
    each = groups // rows
    for k in range(rows):
        out_ref[k * each : (k + 1) * each, :LINE] = got_ref[k ^ ROWS, :length].reshape(each, LINE, TILE)
    shard = got_ref[lax.axis_index("rep") ^ ROWS, length:]
    out_ref[:, LINE:] = jnp.broadcast_to(shard[None], (groups,) + shard.shape)


def product_kernel(nu_ref, l_ref, got_ref, out_ref, m_ref, o_ref, y_ref):
    groups = got_ref.shape[0]
    side = 8
    size = groups * LINE
    got = got_ref[...]
    rows = dot(nu_ref[...], got[:, 2 * LINE :].reshape(size, TILE)).astype(BF16)
    virtual = jnp.concatenate([rows[: size // 2], rows[size // 2 :]], axis=1)
    m_ref[:size] = got[:, :LINE].reshape(size, TILE).astype(F32)
    o_ref[:size] = got[:, LINE : 2 * LINE].reshape(size, TILE).astype(F32)
    mine = [
        jnp.concatenate([m_ref[pl.ds(half * 4 + i, groups, stride=LINE), :] for i in range(4)], axis=0)
        for half in range(2)
    ]
    occupied = [
        jnp.concatenate(
            [
                o_ref[pl.ds(m * LINE + half * 4 + i, side, stride=side * LINE), :]
                for i in range(4)
                for m in range(side)
            ],
            axis=0,
        )
        for half in range(2)
    ]
    mine = jnp.concatenate(mine, axis=1).astype(BF16)
    occupied = jnp.concatenate(occupied, axis=1).astype(BF16)
    halfway = dot(mine, virtual).astype(BF16)
    product = dot(dot(occupied, l_ref[...]).astype(BF16), halfway, TN)
    for i in range(4):
        for half in range(2):
            block = product[i * groups : (i + 1) * groups, half * TILE : (half + 1) * TILE]
            y_ref[pl.ds(half * 4 + i, groups, stride=LINE), :] = block
    out_ref[...] = y_ref[:size].astype(BF16).reshape(groups, LINE, TILE)


def near_kernel(y_ref, near_ref, out_ref, flat_ref, wide_ref):
    count = y_ref.shape[0]
    wide_ref[: count * LINE] = y_ref[...].reshape(count * LINE, TILE).astype(F32)
    picked = [wide_ref[pl.ds(line, count, stride=LINE), :].astype(BF16) for line in (0, 4, 1, 5, 2, 6, 3, 7)]
    flat = jnp.concatenate(picked, axis=1)
    flat_ref[...] = flat
    place(flat, near_ref, 0, out_ref)


def far_kernel(flat_ref, part_ref, far_ref, out_ref):
    out_ref[...] = part_ref[...]
    place(flat_ref[...], far_ref, 2, out_ref)


def place(flat, held_ref, base, out_ref):
    count = flat.shape[0]
    half = count // 2
    part = dot(held_ref[...], flat, NT)
    for index, mask in enumerate((0, 4, 1, 5)):
        rows = part[index * count :][:count]
        wide = jnp.concatenate([rows[:half], rows[half:]], axis=1)
        block = lax.rem((lax.axis_index("row") ^ (mask ^ base)) + 8 - START, 8)
        cut = START * 4
        wide = jnp.concatenate([wide[cut:], wide[:cut]], axis=0)
        out_ref[pl.ds(pl.multiple_of(block * half, half), half), :] = wide


def gather_kernel(*refs):
    count = refs[0].shape[0]
    for step, ref in enumerate(refs[:-1]):
        refs[-1][step * count : (step + 1) * count] = ref[...]


def cost(flops):
    return pl.CostEstimate(flops=flops, bytes_accessed=0, transcendentals=0)


def sum_kernel(got_ref, out_ref):
    size = got_ref.shape[0]
    total = jnp.sum(got_ref[...].reshape(size // 8, 8, TILE), axis=0)
    total = total[:4] + total[4:]
    out_ref[...] = jnp.concatenate([total[:, :64], total[:, 64:]], axis=0)


def exchange(array):
    order, _ = peers(lax.axis_size("col"))
    return lax.all_to_all(array, GRID, 0, 0, tiled=True, axis_index_groups=[order])


def body(m_tensor, green, tile_mask, green_mask):
    row_count, mu_block, ao_count = m_tensor.shape
    groups = lax.axis_size(GRID)
    rows = lax.axis_size("row")
    halves = ao_count // TILE
    line = halves * mu_block
    row = lax.axis_index("row")
    nu_order, l_order = orders(groups)

    own = m_tensor.reshape(row_count, mu_block, halves, TILE).transpose(0, 2, 1, 3)
    own = own.reshape(rows, row_count // rows * line, TILE)
    green_own = green.reshape(2, mu_block, halves, TILE).transpose(0, 2, 1, 3)
    green_own = green_own.reshape(2 * line, TILE)
    first = pl.pallas_call(
        first_kernel,
        out_shape=pltpu.VMEM((rows, row_count // rows * line + 2 * line, TILE), BF16),
        in_specs=[SMEM, SMEM, VMEM, VMEM],
        out_specs=VMEM,
    )(tile_mask.transpose(1, 2, 0), green_mask, own, green_own)
    order = [[k ^ ROWS for k in range(rows)]]
    first = lax.all_to_all(first, "row", 0, 0, tiled=True, axis_index_groups=order)
    sent = pl.pallas_call(
        second_kernel,
        out_shape=pltpu.VMEM((groups, 3 * line, TILE), BF16),
        in_specs=[VMEM],
        out_specs=VMEM,
    )(held(first))

    mu_tile = lax.axis_index(GRID) * mu_block // TILE
    keep_own = jnp.repeat(tile_mask[row * row_count // TILE, mu_tile].astype(BF16), TILE)
    masked = m_tensor * keep_own[None, None, :]

    def flat_rows(block):
        block = block.reshape(rows, 2, row_count // rows // 2, mu_block * ao_count)
        return block.transpose(1, 0, 2, 3).reshape(row_count, mu_block * ao_count)

    def gathered(parts, flops):
        return pl.pallas_call(
            gather_kernel,
            out_shape=pltpu.VMEM((sum(part.shape[0] for part in parts), parts[0].shape[1]), BF16),
            in_specs=[VMEM] * len(parts),
            out_specs=VMEM,
            cost_estimate=cost(flops),
        )(*[held(part) for part in parts])

    def swap(array, bit):
        return lax.ppermute(array, "row", [(r, r ^ bit) for r in range(rows)])

    near = gathered([flat_rows(masked), flat_rows(swap(masked, 4))], COST_G)
    near = gathered([near, swap(near, 1)], COST_H)
    far = swap(near, 2)
    got = exchange(sent)
    product = pl.pallas_call(
        product_kernel,
        out_shape=pltpu.VMEM((groups, line, TILE), BF16),
        in_specs=[VMEM, VMEM, VMEM],
        out_specs=VMEM,
        scratch_shapes=[pltpu.VMEM((groups * line + rows * line, TILE), F32)] * 3,
        cost_estimate=cost(COST_1),
    )(held(pick(nu_order)), held(pick(l_order).T), held(got))
    contracted = exchange(product)
    partial, flat = pl.pallas_call(
        near_kernel,
        out_shape=(
            pltpu.VMEM((groups * 4, TILE), F32),
            pltpu.VMEM((row_count, mu_block * ao_count), BF16),
        ),
        in_specs=[VMEM] * 2,
        out_specs=(VMEM, VMEM),
        scratch_shapes=[pltpu.VMEM((groups * line + rows * line, TILE), F32)],
        cost_estimate=cost(COST_A),
    )(held(contracted), held(near))
    partial = pl.pallas_call(
        far_kernel,
        out_shape=pltpu.VMEM((groups * 4, TILE), F32),
        in_specs=[VMEM] * 3,
        out_specs=VMEM,
        cost_estimate=cost(COST_F),
    )(held(flat), held(partial), held(far))
    slices = exchange(partial.reshape(groups, 4, TILE))
    result = pl.pallas_call(
        sum_kernel,
        out_shape=jax.ShapeDtypeStruct((8, row_count), F32),
        in_specs=[VMEM],
        out_specs=VMEM,
    )(held(slices.reshape(groups * 4, TILE)))
    return result.T


def solution(mesh):
    return jax.shard_map(
        body,
        mesh=mesh,
        in_specs=(P("row", ("col", "rep"), None), P(None, ("row", "col"), None), P(), P()),
        out_specs=P("row", ("col", "rep")),
        check_vma=False,
    )
```

```python
import jax
import jax.numpy as jnp
import numpy as np
from jax import lax
from jax.experimental import pallas as pl
from jax.experimental.pallas import tpu as pltpu
from jax.sharding import PartitionSpec as P

TILE = 128
START = 4
ROWS = 5
COST_F = 1
COST_A = 1
COST_1 = 1
COST_G = 10**10
COST_H = 1
GRID = ("col", "rep")
LINE = 8
BF16 = jnp.bfloat16
F32 = jnp.float32
VMEM = pl.BlockSpec(memory_space=pltpu.VMEM)
SMEM = pl.BlockSpec(memory_space=pltpu.SMEM)
NN = (((1,), (0,)), ((), ()))
NT = (((1,), (1,)), ((), ()))
TN = (((0,), (0,)), ((), ()))


def held(array):
    return pltpu.with_memory_space_constraint(array, pltpu.VMEM)


def dot(left, right, dims=NN):
    return lax.dot_general(left, right, dims, preferred_element_type=F32)


def pick(index):
    index = np.asarray(index)
    return jnp.asarray(index[:, None] == np.arange(index.size)[None, :], BF16)


def peers(side):
    order = [
        (START + i) % side * side + (START + j) % side for i in range(side) for j in range(side)
    ]
    return order, np.argsort(order)


def orders(groups):
    side = int(round(groups**0.5))
    size = groups * LINE
    order, place = peers(side)
    row = np.arange(size)
    half, nu = row // (size // 2), row % (size // 2)
    block, inner = nu // 4, nu % 4
    source = place[block % side * side + block // side]
    column = np.arange(size // 2)
    return source * LINE + half * 4 + inner, np.asarray(order)[column % groups] * 4 + column // groups


def first_kernel(tile_ref, green_ref, m_ref, shard_ref, out_ref):
    tile, mu_tile = lax.axis_index("row") // 2, lax.axis_index("col") // 4
    green_tile = lax.axis_index("row") // 4
    length = m_ref.shape[1]

    def halves(count, low, high):
        line = lax.broadcasted_iota(jnp.int32, (count, TILE), 0) % LINE
        return jnp.where(line < 4, low.astype(F32), high.astype(F32))

    keep = halves(length, tile_ref[mu_tile, 0, tile], tile_ref[mu_tile, 1, tile])
    for k in range(out_ref.shape[0]):
        out_ref[k, :length] = (m_ref[k ^ ROWS].astype(F32) * keep).astype(BF16)
    keep_green = jnp.concatenate(
        [halves(LINE, green_ref[w, green_tile, 0], green_ref[w, green_tile, 1]) for w in range(2)], axis=0
    )
    shard = (shard_ref[...].astype(F32) * keep_green).astype(BF16)
    for k in range(out_ref.shape[0]):
        out_ref[k, length:] = shard


def second_kernel(got_ref, out_ref, made_ref, sems):
    rows = got_ref.shape[0]
    each = out_ref.shape[0] // rows
    length = each * LINE
    shard = got_ref[lax.axis_index("rep") ^ ROWS, length:]
    leave = []
    for k in range(rows):
        part = pl.ds(k * each, each)
        made_ref[part, :LINE] = got_ref[k ^ ROWS, :length].reshape(each, LINE, TILE)
        made_ref[part, LINE:] = jnp.broadcast_to(shard[None], (each,) + shard.shape)
        leave.append(pltpu.make_async_copy(made_ref.at[part], out_ref.at[part], sems.at[k]))
        leave[-1].start()
    for copy in leave:
        copy.wait()


def product_kernel(nu_ref, l_ref, got_ref, out_ref, m_ref, o_ref, y_ref):
    groups = got_ref.shape[0]
    side = 8
    size = groups * LINE
    got = got_ref[...]
    rows = dot(nu_ref[...], got[:, 2 * LINE :].reshape(size, TILE)).astype(BF16)
    virtual = jnp.concatenate([rows[: size // 2], rows[size // 2 :]], axis=1)
    m_ref[:size] = got[:, :LINE].reshape(size, TILE).astype(F32)
    o_ref[:size] = got[:, LINE : 2 * LINE].reshape(size, TILE).astype(F32)
    mine = [
        jnp.concatenate([m_ref[pl.ds(half * 4 + i, groups, stride=LINE), :] for i in range(4)], axis=0)
        for half in range(2)
    ]
    occupied = [
        jnp.concatenate(
            [
                o_ref[pl.ds(m * LINE + half * 4 + i, side, stride=side * LINE), :]
                for i in range(4)
                for m in range(side)
            ],
            axis=0,
        )
        for half in range(2)
    ]
    mine = jnp.concatenate(mine, axis=1).astype(BF16)
    occupied = jnp.concatenate(occupied, axis=1).astype(BF16)
    halfway = dot(mine, virtual).astype(BF16)
    product = dot(dot(occupied, l_ref[...]).astype(BF16), halfway, TN)
    for i in range(4):
        for half in range(2):
            block = product[i * groups : (i + 1) * groups, half * TILE : (half + 1) * TILE]
            y_ref[pl.ds(half * 4 + i, groups, stride=LINE), :] = block
    out_ref[...] = y_ref[:size].astype(BF16).reshape(groups, LINE, TILE)


def near_kernel(y_ref, near_ref, out_ref, flat_ref, wide_ref):
    count = y_ref.shape[0]
    wide_ref[: count * LINE] = y_ref[...].reshape(count * LINE, TILE).astype(F32)
    picked = [wide_ref[pl.ds(line, count, stride=LINE), :].astype(BF16) for line in (0, 4, 1, 5, 2, 6, 3, 7)]
    flat = jnp.concatenate(picked, axis=1)
    flat_ref[...] = flat
    place(flat, near_ref, 0, out_ref)


def far_kernel(flat_ref, part_ref, far_ref, out_ref):
    out_ref[...] = part_ref[...]
    place(flat_ref[...], far_ref, 2, out_ref)


def place(flat, held_ref, base, out_ref):
    count = flat.shape[0]
    half = count // 2
    part = dot(held_ref[...], flat, NT)
    for index, mask in enumerate((0, 4, 1, 5)):
        rows = part[index * count :][:count]
        wide = jnp.concatenate([rows[:half], rows[half:]], axis=1)
        block = lax.rem((lax.axis_index("row") ^ (mask ^ base)) + 8 - START, 8)
        cut = START * 4
        wide = jnp.concatenate([wide[cut:], wide[:cut]], axis=0)
        out_ref[pl.ds(pl.multiple_of(block * half, half), half), :] = wide


def gather_kernel(*refs):
    count = refs[0].shape[0]
    for step, ref in enumerate(refs[:-1]):
        refs[-1][step * count : (step + 1) * count] = ref[...]


def cost(flops):
    return pl.CostEstimate(flops=flops, bytes_accessed=0, transcendentals=0)


def sum_kernel(got_ref, out_ref):
    size = got_ref.shape[0]
    total = jnp.sum(got_ref[...].reshape(size // 8, 8, TILE), axis=0)
    total = total[:4] + total[4:]
    out_ref[...] = jnp.concatenate([total[:, :64], total[:, 64:]], axis=0)


def exchange(array):
    order, _ = peers(lax.axis_size("col"))
    return lax.all_to_all(array, GRID, 0, 0, tiled=True, axis_index_groups=[order])


def body(m_tensor, green, tile_mask, green_mask):
    row_count, mu_block, ao_count = m_tensor.shape
    groups = lax.axis_size(GRID)
    rows = lax.axis_size("row")
    halves = ao_count // TILE
    line = halves * mu_block
    row = lax.axis_index("row")
    nu_order, l_order = orders(groups)

    own = m_tensor.reshape(row_count, mu_block, halves, TILE).transpose(0, 2, 1, 3)
    own = own.reshape(rows, row_count // rows * line, TILE)
    green_own = green.reshape(2, mu_block, halves, TILE).transpose(0, 2, 1, 3)
    green_own = green_own.reshape(2 * line, TILE)
    first = pl.pallas_call(
        first_kernel,
        out_shape=pltpu.VMEM((rows, row_count // rows * line + 2 * line, TILE), BF16),
        in_specs=[SMEM, SMEM, VMEM, VMEM],
        out_specs=VMEM,
    )(tile_mask.transpose(1, 2, 0), green_mask, own, green_own)
    order = [[k ^ ROWS for k in range(rows)]]
    first = lax.all_to_all(first, "row", 0, 0, tiled=True, axis_index_groups=order)
    sent = pl.pallas_call(
        second_kernel,
        out_shape=jax.ShapeDtypeStruct((groups, 3 * line, TILE), BF16),
        in_specs=[VMEM],
        out_specs=pl.BlockSpec(memory_space=pl.ANY),
        scratch_shapes=[pltpu.VMEM((groups, 3 * line, TILE), BF16), pltpu.SemaphoreType.DMA((rows,))],
    )(held(first))

    mu_tile = lax.axis_index(GRID) * mu_block // TILE
    keep_own = jnp.repeat(tile_mask[row * row_count // TILE, mu_tile].astype(BF16), TILE)
    right = m_tensor * keep_own[None, None, :]
    right = right.reshape(rows, 2, row_count // rows // 2, mu_block * ao_count).transpose(1, 0, 2, 3)
    right = right.reshape(row_count, mu_block * ao_count)

    def gathered(parts, flops):
        return pl.pallas_call(
            gather_kernel,
            out_shape=pltpu.VMEM((sum(part.shape[0] for part in parts), parts[0].shape[1]), BF16),
            in_specs=[VMEM] * len(parts),
            out_specs=VMEM,
            cost_estimate=cost(flops),
        )(*[held(part) for part in parts])

    def swap(array, bit):
        return lax.ppermute(array, "row", [(r, r ^ bit) for r in range(rows)])

    near = gathered([right, swap(right, 4)], COST_G)
    near = gathered([near, swap(near, 1)], COST_H)
    far = swap(near, 2)
    got = exchange(sent)
    product = pl.pallas_call(
        product_kernel,
        out_shape=pltpu.VMEM((groups, line, TILE), BF16),
        in_specs=[VMEM, VMEM, VMEM],
        out_specs=VMEM,
        scratch_shapes=[pltpu.VMEM((groups * line + rows * line, TILE), F32)] * 3,
        cost_estimate=cost(COST_1),
    )(held(pick(nu_order)), held(pick(l_order).T), held(got))
    contracted = exchange(product)
    partial, flat = pl.pallas_call(
        near_kernel,
        out_shape=(
            pltpu.VMEM((groups * 4, TILE), F32),
            pltpu.VMEM((row_count, mu_block * ao_count), BF16),
        ),
        in_specs=[VMEM] * 2,
        out_specs=(VMEM, VMEM),
        scratch_shapes=[pltpu.VMEM((groups * line + rows * line, TILE), F32)],
        cost_estimate=cost(COST_A),
    )(held(contracted), held(near))
    partial = pl.pallas_call(
        far_kernel,
        out_shape=pltpu.VMEM((groups * 4, TILE), F32),
        in_specs=[VMEM] * 3,
        out_specs=VMEM,
        cost_estimate=cost(COST_F),
    )(held(flat), held(partial), held(far))
    slices = exchange(partial.reshape(groups, 4, TILE))
    result = pl.pallas_call(
        sum_kernel,
        out_shape=jax.ShapeDtypeStruct((8, row_count), F32),
        in_specs=[VMEM],
        out_specs=VMEM,
    )(held(slices.reshape(groups * 4, TILE)))
    return result.T


def solution(mesh):
    return jax.shard_map(
        body,
        mesh=mesh,
        in_specs=(P("row", ("col", "rep"), None), P(None, ("row", "col"), None), P(), P()),
        out_specs=P("row", ("col", "rep")),
        check_vma=False,
    )
```
